32 devices in a mesh: rows: 8 (over y, x, core), seq: 4 (over z).
Axes of the slice: x: 2, y: 2, z: 4, core: 2. Of those that a mesh axis runs over, the one named last changes fastest.
Arguments:
- inputs: bfloat16 [8, 1024, 2048], P('rows', 'seq'), may hold values from -6 to 6
- cotangent: bfloat16 [8, 1024, 2048], P('rows', 'seq'), may hold values from -6 to 6
- doc_lengths: int32 [8, 2], P('rows'), may hold values from 1 to 896, 1024 in all within a row
- gain_attn: bfloat16 [2048], P(('rows', 'seq')), may hold values from 0.5 to 1.5
- w_query: bfloat16 [2048, 2048], P(('rows', 'seq')), may hold values from -0.125 to 0.125
- w_key: bfloat16 [2048, 512], P(('rows', 'seq')), may hold values from -0.125 to 0.125
- w_value: bfloat16 [2048, 512], P(('rows', 'seq')), may hold values from -0.125 to 0.125
- w_out: bfloat16 [2048, 2048], P(('rows', 'seq')), may hold values from -2 to 2
- gain_mlp: bfloat16 [2048], P(('rows', 'seq')), may hold values from 0.5 to 1.5
- w_gate: bfloat16 [2048, 8192], P(('rows', 'seq')), may hold values from -0.125 to 0.125
- w_up: bfloat16 [2048, 8192], P(('rows', 'seq')), may hold values from -0.125 to 0.125
- w_down: bfloat16 [8192, 2048], P(('rows', 'seq')), may hold values from -0.0625 to 0.0625
Outputs:
- layer_out: bfloat16 [8, 1024, 2048], P('rows', 'seq')
- input_grad: bfloat16 [8, 1024, 2048], P('rows', 'seq')
- gain_attn_grad: float32 [2048], P(('rows', 'seq'))
- query_grad: float32 [2048, 2048], P(('rows', 'seq'))
- key_grad: float32 [2048, 512], P(('rows', 'seq'))
- value_grad: float32 [2048, 512], P(('rows', 'seq'))
- out_grad: float32 [2048, 2048], P(('rows', 'seq'))
- gain_mlp_grad: float32 [2048], P(('rows', 'seq'))
- gate_grad: float32 [2048, 8192], P(('rows', 'seq'))
- up_grad: float32 [2048, 8192], P(('rows', 'seq'))
- down_grad: float32 [8192, 2048], P(('rows', 'seq'))
The draws below stay inside these ranges and needn't reach their ends.
Inputs may be any that keep to these rules, and one draw needn't show every extreme that they name: `doc_lengths`: each row's 2 document lengths sum to 1024, and the longest of every row is at most 896.
All inputs are finite; a program needn't handle non-finite values.
Results may differ from the reference program's by a relative error of at most 0.014.
Values may be sent and summed in bfloat16 or wider, within the bound.
No kernel may reach another device: no remote copies, remote signals or barrier semaphores. Data moves between devices by JAX's collectives and lax.ppermute only.
A program may use at most 640 MiB of HBM per device.

```python
import math
import jax
import jax.numpy as jnp
import numpy as np
from jax import lax

D = 2048
HEADS = 32
KV_HEADS = 8
HEAD_DIM = 64
FF = 8192
NDOC = 2
ROW_LEN = 1024
ROWS = 8
MOST_DOC = 896


def block_levels(own_key, dims, shards, low, high):
    def one(dim, parts):
        heights = jax.random.uniform(jax.random.fold_in(jax.random.fold_in(own_key, 6), dim), (parts,), jnp.float32, low / len(shards), high / len(shards))
        return jnp.repeat(jnp.exp(heights), dims[dim] // parts).reshape((-1,) + (1,) * (len(dims) - dim - 1))

    factor_of = one(*shards[0])
    for cut in shards[1:]:
        factor_of = factor_of * one(*cut)
    return factor_of


def profile(number_of, total, limit, slope):
    loads = [(1 << 20) // math.isqrt(rank ** slope) + 1 for rank in range(2, number_of + 1)]
    rest, holding = total - limit - (number_of - 1), [1] * (number_of - 1)
    while rest > 0:
        free = [i for i in range(number_of - 1) if holding[i] < limit]
        pool, budget = sum([loads[i] for i in free]), rest
        for i in free:
            addition = min(limit - holding[i], max(1, budget * loads[i] // pool), rest)
            holding[i] = holding[i] + addition
            rest = rest - addition
    return np.array([limit] + holding)


def uneven(key, count, total, reach, lean):
    if count == 2:
        one = jax.random.randint(key, (), max(1, total - reach), min(reach, total - 1) + 1)
        return jnp.stack([one, total - one])
    tallies = jnp.asarray(profile(count, total, reach, lean), jnp.int32)
    twos = (count - 1) // 2
    source_of, receiver = tallies[1:1 + 2 * twos:2], tallies[2:2 + 2 * twos:2]
    margin = jnp.minimum(source_of - 1, reach - receiver)
    passed = jax.random.randint(jax.random.fold_in(key, 1), (twos,), 0, 1 << 20) % (margin + 1)
    tallies = tallies.at[1:1 + 2 * twos:2].set(source_of - passed).at[2:2 + 2 * twos:2].set(receiver + passed)
    return tallies[jax.random.permutation(jax.random.fold_in(key, 2), count)]


def scatter_about(own_key, shape, scale, reach, pieces=(), kind=jnp.bfloat16):
    gain = block_levels(own_key, shape, pieces, -0.22, 0.18) if pieces else 1.0
    entries = jax.random.normal(own_key, shape, jnp.float32) * scale * gain
    return jnp.minimum(jnp.maximum(entries, -reach), reach).astype(kind)


def setup_inputs(seed: int = 0) -> dict:
    key_of = jax.random.split(jax.random.key(seed), 13)
    return {
        "inputs": scatter_about(key_of[0], (ROWS, ROW_LEN, D), 1.0, 6.0, ((0, 8), (1, 4))),
        "cotangent": scatter_about(key_of[1], (ROWS, ROW_LEN, D), 1.0, 6.0, ((0, 8), (1, 4))),
        "doc_lengths": jax.vmap(lambda own: uneven(own, NDOC, ROW_LEN, MOST_DOC, 2))(jax.random.split(key_of[2], ROWS)).reshape((ROWS, NDOC)).astype(jnp.int32),
        "gain_attn": jnp.clip(1.0 + 0.1 * jax.random.normal(key_of[3], (D,), jnp.float32), 0.5, 1.5).astype(jnp.bfloat16),
        "w_query": scatter_about(key_of[4], (D, HEADS * HEAD_DIM), D ** -0.5, 0.125, ((0, 32),)),
        "w_key": scatter_about(key_of[5], (D, KV_HEADS * HEAD_DIM), D ** -0.5, 0.125, ((0, 32),)),
        "w_value": scatter_about(key_of[6], (D, KV_HEADS * HEAD_DIM), D ** -0.5, 0.125, ((0, 32),)),
        "w_out": scatter_about(key_of[7], (HEADS * HEAD_DIM, D), (HEADS * HEAD_DIM // 256) ** -0.5, 2.0, ((0, 32),)),
        "gain_mlp": jnp.clip(1.0 + 0.1 * jax.random.normal(key_of[8], (D,), jnp.float32), 0.5, 1.5).astype(jnp.bfloat16),
        "w_gate": scatter_about(key_of[9], (D, FF), D ** -0.5, 0.125, ((0, 32),)),
        "w_up": scatter_about(key_of[10], (D, FF), D ** -0.5, 0.125, ((0, 32),)),
        "w_down": scatter_about(key_of[11], (FF, D), FF ** -0.5, 0.0625, ((0, 32),)),
    }


epsilon = 1e-05
rope_theta = 500000.0
masked_score = -1e+30

@jax.custom_vjp
def low(v):
    return lax.optimization_barrier(v.astype(jnp.bfloat16)).astype(jnp.float32)

@jax.custom_vjp
def low_back(v):
    return v

def low_keep(v):
    return (low(v), None)

def low_pass(kept, grad):
    return (grad,)

def back_keep(v):
    return (v, None)

def back_low(kept, grad):
    return (low(grad),)
low.defvjp(low_keep, low_pass)
low_back.defvjp(back_keep, back_low)

def rope_table(head_width):
    listed = []
    for column in range(head_width // 2):
        natural = rope_theta ** (-2.0 * column / head_width)
        wavelength = 2.0 * math.pi / natural
        if wavelength > 8192.0:
            scaled = natural / 32.0
        elif wavelength < 2048.0:
            scaled = natural
        else:
            blending = (8192.0 / wavelength - 1.0) / 3.0
            scaled = (1.0 - blending) * natural / 32.0 + blending * natural
        listed.append(scaled)
    return jnp.asarray(listed + listed, dtype=jnp.float32)

def rms_scale(values):
    return lax.rsqrt(lax.optimization_barrier(jnp.mean(values * values, axis=-1, keepdims=True)) + epsilon)

def rotate(values, cosine, sine_table):
    halfway = values.shape[-1] // 2
    turned = jnp.concatenate([-values[..., halfway:], values[..., :halfway]], axis=-1)
    return values * cosine + turned * sine_table

def dense_high(left_side, right_side):
    return jnp.dot(left_side, right_side, precision=lax.Precision.HIGHEST, preferred_element_type=jnp.float32)

def attention(queries, keys_all, values_all, token_start):
    places = jnp.arange(ROW_LEN, dtype=jnp.int32)
    allowed = (places[None, :] <= places[:, None]) & (places[None, :] >= token_start[:, None])
    repeats = HEADS // KV_HEADS
    keys_wide = jnp.repeat(keys_all, repeats, axis=1)
    values_wide = jnp.repeat(values_all, repeats, axis=1)

    def one_head(operands):
        head_query, head_key, head_value = operands
        scores = low_back(dense_high(head_query, head_key.T) * HEAD_DIM ** (-0.5))
        scores = jnp.where(allowed, scores, masked_score)
        highest = lax.optimization_barrier(jnp.max(scores, axis=-1, keepdims=True))
        exponent = jnp.exp(scores - highest)
        weights = low(exponent / lax.optimization_barrier(jnp.sum(exponent, axis=-1, keepdims=True)))
        return dense_high(weights, head_value)
    outputs = lax.map(jax.checkpoint(one_head), (jnp.transpose(queries, (1, 0, 2)), jnp.transpose(keys_wide, (1, 0, 2)), jnp.transpose(values_wide, (1, 0, 2))))
    return jnp.transpose(outputs, (1, 0, 2)).reshape(ROW_LEN, HEADS * HEAD_DIM)

def layer_forward(params, inputs_row, token_start, cosine, sine_table):
    gain_attn, w_query, w_key, w_value, w_out, gain_mlp, w_gate, w_up, w_down = params
    normed = low(inputs_row * rms_scale(inputs_row) * gain_attn)
    shaped_q = low_back(dense_high(normed, w_query)).reshape(ROW_LEN, HEADS, HEAD_DIM)
    queries = low_back(low(rotate(shaped_q, cosine, sine_table)))
    shaped_k = low_back(dense_high(normed, w_key)).reshape(ROW_LEN, KV_HEADS, HEAD_DIM)
    keys_all = low_back(low(rotate(shaped_k, cosine, sine_table)))
    values_all = low_back(low(dense_high(normed, w_value))).reshape(ROW_LEN, KV_HEADS, HEAD_DIM)
    attended = low_back(low(attention(queries, keys_all, values_all, token_start)))
    hidden_one = inputs_row + low_back(dense_high(attended, w_out))
    normed_two = low(hidden_one * rms_scale(hidden_one) * gain_mlp)
    gate_value = low_back(dense_high(normed_two, w_gate))
    upward = low_back(dense_high(normed_two, w_up))
    inner_act = low(gate_value * jax.nn.sigmoid(gate_value) * upward)
    return hidden_one + low_back(dense_high(inner_act, w_down))

def reference(inputs, cotangent, doc_lengths, gain_attn, w_query, w_key, w_value, w_out, gain_mlp, w_gate, w_up, w_down):
    params = tuple((weight.astype(jnp.float32) for weight in (gain_attn, w_query, w_key, w_value, w_out, gain_mlp, w_gate, w_up, w_down)))
    frequency = rope_table(HEAD_DIM)
    places = jnp.arange(ROW_LEN, dtype=jnp.int32)

    def row_step(totals, operands):
        row_input, row_cotangent, row_lengths = operands
        doc_ends = jnp.cumsum(row_lengths).astype(jnp.int32)
        doc_starts = (doc_ends - row_lengths).astype(jnp.int32)
        inside = (places[:, None] >= doc_starts[None, :]) & (places[:, None] < doc_ends[None, :])
        token_start = lax.optimization_barrier(jnp.sum(jnp.where(inside, doc_starts[None, :], 0), axis=1)).astype(jnp.int32)
        angles = (places - token_start).astype(jnp.float32)[:, None] * frequency[None, :]
        cosine = jnp.cos(angles)[:, None, :]
        sine_table = jnp.sin(angles)[:, None, :]

        def forward(inputs_row, weights_all):
            return layer_forward(weights_all, inputs_row, token_start, cosine, sine_table)
        result, pullback = jax.vjp(forward, row_input.astype(jnp.float32), params)
        grad_input, weight_grads = pullback(row_cotangent.astype(jnp.float32))
        totals = jax.tree.map(jnp.add, totals, weight_grads)
        return (totals, (result.astype(jnp.bfloat16), grad_input.astype(jnp.bfloat16)))
    initial = jax.tree.map(jnp.zeros_like, params)
    totals, (layer_out, input_grad) = lax.scan(row_step, initial, (inputs, cotangent, doc_lengths))
    gain_attn_grad, query_grad, key_grad, value_grad, out_grad, gain_mlp_grad, gate_grad, up_grad, down_grad = totals
    return (layer_out, input_grad, gain_attn_grad, query_grad, key_grad, value_grad, out_grad, gain_mlp_grad, gate_grad, up_grad, down_grad)
```

```python
import math

import jax
import jax.numpy as jnp
from jax import lax
from jax.sharding import PartitionSpec as P

HEAD_DIM = 64


epsilon = 1e-05
rope_theta = 500000.0
masked_score = -1e30


def rope_table(head_width):
    listed = []
    for column in range(head_width // 2):
        natural = rope_theta ** (-2.0 * column / head_width)
        wavelength = 2.0 * math.pi / natural
        if wavelength > 8192.0:
            scaled = natural / 32.0
        elif wavelength < 2048.0:
            scaled = natural
        else:
            blending = (8192.0 / wavelength - 1.0) / 3.0
            scaled = (1.0 - blending) * natural / 32.0 + blending * natural
        listed.append(scaled)
    return jnp.asarray(listed + listed, dtype=jnp.float32)


def rms_scale(values):
    return lax.rsqrt(jnp.mean(values * values, axis=-1, keepdims=True) + epsilon)


def rotate(values, cosine, sine_table):
    halfway = values.shape[-1] // 2
    turned = jnp.concatenate([-values[..., halfway:], values[..., :halfway]], axis=-1)
    return values * cosine + turned * sine_table


def rotate_back(values, cosine, sine_table):
    halfway = values.shape[-1] // 2
    turned = jnp.concatenate([values[..., halfway:], -values[..., :halfway]], axis=-1)
    return values * cosine + turned * sine_table


def dense_low(left_side, right_side):
    return jnp.dot(left_side, right_side, preferred_element_type=jnp.float32)


def against_rows(left_side, right_side):
    return lax.dot_general(
        left_side, right_side, (((1,), (1,)), ((), ())), preferred_element_type=jnp.float32
    )


def across_tokens(left_side, right_side):
    return lax.dot_general(
        left_side, right_side, (((0,), (0,)), ((), ())), preferred_element_type=jnp.float32
    )


def norm_back(grad_normed, normed_unit, scale_rows, gain_full):
    scaled_grad = grad_normed * gain_full
    return scale_rows * (
        scaled_grad - normed_unit * jnp.mean(scaled_grad * normed_unit, axis=-1, keepdims=True)
    )


def ring_gather(own, axis):
    count = lax.axis_size(axis)
    here = lax.axis_index(axis)
    onward = [(i, (i + 1) % count) for i in range(count)]
    block = own
    out = jnp.zeros((count,) + own.shape, own.dtype)
    out = lax.dynamic_update_index_in_dim(out, block, here, 0)
    for hop in range(1, count):
        block = lax.ppermute(block, axis, onward)
        out = lax.dynamic_update_index_in_dim(out, block, (here - hop + count) % count, 0)
    return out


def ring_reduce(parts, axis):
    count = lax.axis_size(axis)
    here = lax.axis_index(axis)
    onward = [(i, (i + 1) % count) for i in range(count)]

    def part(back):
        return lax.dynamic_index_in_dim(parts, (here - back + 2 * count) % count, 0, keepdims=False)

    total = part(1).astype(jnp.bfloat16)
    for hop in range(1, count):
        arrived = lax.ppermute(total, axis, onward).astype(jnp.float32)
        total = arrived + part(1 + hop).astype(jnp.float32)
        if hop < count - 1:
            total = total.astype(jnp.bfloat16)
    return total


def local(
    inputs,
    cotangent,
    doc_lengths,
    gain_attn,
    w_query,
    w_key,
    w_value,
    w_out,
    gain_mlp,
    w_gate,
    w_up,
    w_down,
):
    seq_count = lax.axis_size("seq")
    row_count = lax.axis_size("rows")
    local_len = inputs.shape[1]
    width = inputs.shape[2]
    row_len = local_len * seq_count
    head_scale = HEAD_DIM ** (-0.5)
    q_cols, kv_cols = w_query.shape[1], w_key.shape[1]
    both = ("rows", "seq")
    low = jnp.bfloat16

    gains = jnp.stack([gain_attn, gain_mlp], axis=1)
    gains = jnp.pad(gains, ((0, 0), (0, 126)))
    attn_local = jnp.concatenate([w_query, w_key, w_value, gains], axis=1)
    attn_full = lax.all_gather(attn_local, both, axis=0, tiled=True)
    out_full = lax.all_gather(w_out, both, axis=0, tiled=True)
    qkv_full = attn_full[:, : q_cols + 2 * kv_cols]
    gain_cols = attn_full[:, q_cols + 2 * kv_cols :].T
    gain_one = gain_cols[0].astype(jnp.float32)
    gain_two = gain_cols[1].astype(jnp.float32)

    gate_up_slab = lax.all_to_all(
        jnp.stack([w_gate.reshape(-1, row_count, w_gate.shape[1] // row_count),
                   w_up.reshape(-1, row_count, w_up.shape[1] // row_count)], axis=2),
        "rows", split_axis=1, concat_axis=0, tiled=True,
    )
    ff_local = w_gate.shape[1] // row_count
    gate_up_slab = gate_up_slab.reshape(row_count, w_gate.shape[0], 2 * ff_local)
    gate_up_full = ring_gather(gate_up_slab, "seq")
    gate_up_full = jnp.transpose(gate_up_full, (1, 0, 2, 3)).reshape(width, 2 * ff_local)
    down_full = ring_gather(w_down, "seq").reshape(ff_local, width)
    grad_tokens = lax.all_gather(cotangent[0], "rows", axis=0, tiled=True)

    places = jnp.arange(row_len, dtype=jnp.int32)
    row_lengths = doc_lengths[0]
    doc_ends = jnp.cumsum(row_lengths)
    doc_starts = doc_ends - row_lengths
    inside = (places[:, None] >= doc_starts[None, :]) & (places[:, None] < doc_ends[None, :])
    token_start = jnp.sum(jnp.where(inside, doc_starts[None, :], 0), axis=1)
    offset = lax.axis_index("seq") * local_len
    local_places = lax.dynamic_slice_in_dim(places, offset, local_len)
    local_start = lax.dynamic_slice_in_dim(token_start, offset, local_len)
    frequency = rope_table(HEAD_DIM)
    angles = (local_places - local_start).astype(jnp.float32)[:, None] * frequency[None, :]
    cosine = jnp.cos(angles)[:, None, :]
    sine_table = jnp.sin(angles)[:, None, :]

    inputs_f = inputs[0].astype(jnp.float32)
    scale_one = rms_scale(inputs_f)
    unit_one = inputs_f * scale_one
    normed = (unit_one * gain_one).astype(low)
    lin = dense_low(normed, qkv_full)
    queries = rotate(lin[:, :q_cols].reshape(local_len, -1, HEAD_DIM), cosine, sine_table).astype(low)
    keys_loc = (
        rotate(lin[:, q_cols : q_cols + kv_cols].reshape(local_len, -1, HEAD_DIM), cosine, sine_table)
        .astype(low)
        .reshape(local_len, kv_cols)
    )
    values_loc = lin[:, q_cols + kv_cols :].astype(low)
    pairs = ring_gather(jnp.concatenate([keys_loc, values_loc], axis=1), "seq")
    pairs = pairs.reshape(row_len, 2 * kv_cols)
    kv_heads = kv_cols // HEAD_DIM
    group_size = q_cols // kv_cols
    keys_grid = pairs[:, :kv_cols].reshape(row_len, kv_heads, HEAD_DIM)
    values_grid = pairs[:, kv_cols:].reshape(row_len, kv_heads, HEAD_DIM)
    query_grid = queries.reshape(local_len, kv_heads, group_size, HEAD_DIM)
    allowed = (places[None, :] <= local_places[:, None]) & (places[None, :] >= local_start[:, None])

    def scores_of():
        scores = (
            jnp.einsum("qgrd,kgd->grqk", query_grid, keys_grid, preferred_element_type=jnp.float32)
            * head_scale
        )
        return jnp.where(allowed, scores, masked_score)

    scores = scores_of()
    highest = jnp.max(scores, axis=-1, keepdims=True)
    exponent = jnp.exp(scores - highest)
    row_total = jnp.sum(exponent, axis=-1, keepdims=True)
    weights = (exponent / row_total).astype(low)
    attended = (
        jnp.einsum("grqk,kgd->qgrd", weights, values_grid, preferred_element_type=jnp.float32)
        .astype(low)
        .reshape(local_len, -1)
    )
    log_total = highest + jnp.log(row_total)

    hidden_one = inputs_f + dense_low(attended, out_full)
    scale_two = rms_scale(hidden_one)
    unit_two = hidden_one * scale_two
    normed_two = (unit_two * gain_two).astype(low)

    tokens = lax.all_gather(normed_two, "rows", axis=0, tiled=True)
    gate_up = dense_low(tokens, gate_up_full)
    gate_value, up_value = gate_up[:, :ff_local], gate_up[:, ff_local:]
    sigmoid_gate = jax.nn.sigmoid(gate_value)
    inner_act = (gate_value * sigmoid_gate * up_value).astype(low)
    grad_inner = against_rows(grad_tokens, down_full)
    grad_up = (grad_inner * gate_value * sigmoid_gate).astype(low)
    grad_gate = (
        grad_inner * up_value * sigmoid_gate * (1.0 + gate_value * (1.0 - sigmoid_gate))
    ).astype(low)
    grad_pair = jnp.concatenate([grad_gate, grad_up], axis=1)
    normed_two_part = against_rows(grad_pair, gate_up_full).astype(low)
    grad_normed_two = lax.psum_scatter(
        normed_two_part, "rows", scatter_dimension=0, tiled=True
    ).astype(jnp.float32)
    mixed_part = dense_low(inner_act, down_full).astype(low)
    mixed = lax.psum_scatter(mixed_part, "rows", scatter_dimension=0, tiled=True)
    layer_out = (hidden_one + mixed.astype(jnp.float32)).astype(low)

    down_part = across_tokens(inner_act, grad_tokens).astype(low)
    down_grad = ring_reduce(down_part.reshape(seq_count, -1, width), "seq")
    gate_up_part = across_tokens(tokens, grad_pair).astype(low)
    gate_up_part = jnp.transpose(
        gate_up_part.reshape(row_count, seq_count, -1, 2 * ff_local), (1, 0, 2, 3)
    )
    gate_up_sum = ring_reduce(gate_up_part, "seq").astype(low)
    gate_up_sum = gate_up_sum.reshape(row_count, -1, 2, ff_local)
    gate_up_back = lax.all_to_all(gate_up_sum, "rows", split_axis=0, concat_axis=0, tiled=True)
    gate_grad = jnp.transpose(gate_up_back[:, :, 0], (1, 0, 2)).reshape(-1, w_gate.shape[1])
    up_grad = jnp.transpose(gate_up_back[:, :, 1], (1, 0, 2)).reshape(-1, w_gate.shape[1])
    gate_grad = gate_grad.astype(jnp.float32)
    up_grad = up_grad.astype(jnp.float32)

    grad_out = cotangent[0].astype(jnp.float32)
    gain_two_part = jnp.sum(grad_normed_two * unit_two, axis=0)
    grad_hidden = grad_out + norm_back(grad_normed_two, unit_two, scale_two, gain_two)
    grad_branch = grad_hidden.astype(low)
    grad_attended = against_rows(grad_branch, out_full).astype(low)
    out_part = across_tokens(attended, grad_branch).astype(low)
    out_sum = lax.psum_scatter(out_part, "rows", scatter_dimension=0, tiled=True)
    out_grad = ring_reduce(out_sum.reshape(seq_count, -1, width), "seq")

    grad_grid = grad_attended.reshape(local_len, kv_heads, group_size, HEAD_DIM)
    probabilities = jnp.exp(scores_of() - log_total)
    weights_b = probabilities.astype(low)
    grad_probs = jnp.einsum(
        "qgrd,kgd->grqk", grad_grid, values_grid, preferred_element_type=jnp.float32
    )
    centre = jnp.sum(probabilities * grad_probs, axis=-1, keepdims=True)
    grad_scores = (probabilities * (grad_probs - centre)).astype(low)
    grad_q = (
        jnp.einsum("grqk,kgd->qgrd", grad_scores, keys_grid, preferred_element_type=jnp.float32)
        * head_scale
    ).astype(low)
    key_part = (
        jnp.einsum("grqk,qgrd->kgd", grad_scores, query_grid, preferred_element_type=jnp.float32)
        * head_scale
    )
    value_part = jnp.einsum(
        "grqk,qgrd->kgd", weights_b, grad_grid, preferred_element_type=jnp.float32
    )
    pair_part = jnp.concatenate(
        [key_part.reshape(row_len, kv_cols), value_part.reshape(row_len, kv_cols)], axis=1
    )
    pair_grad = ring_reduce(pair_part.reshape(seq_count, local_len, 2 * kv_cols), "seq").astype(low)
    lin_q = (
        rotate_back(
            grad_q.astype(jnp.float32).reshape(local_len, -1, HEAD_DIM), cosine, sine_table
        )
        .astype(low)
        .reshape(local_len, q_cols)
    )
    lin_k = (
        rotate_back(
            pair_grad[:, :kv_cols].astype(jnp.float32).reshape(local_len, -1, HEAD_DIM),
            cosine,
            sine_table,
        )
        .astype(low)
        .reshape(local_len, kv_cols)
    )
    lin_kv = jnp.concatenate([lin_k, pair_grad[:, kv_cols:]], axis=1)
    query_part = across_tokens(normed, lin_q).astype(low)
    query_sum = lax.psum_scatter(query_part, "rows", scatter_dimension=0, tiled=True)
    grad_normed = against_rows(lin_q, qkv_full[:, :q_cols]) + against_rows(
        lin_kv, qkv_full[:, q_cols:]
    )
    gain_one_part = jnp.sum(grad_normed * unit_one, axis=0)
    input_grad = (
        grad_hidden + norm_back(grad_normed, unit_one, scale_one, gain_one)
    ).astype(low)
    gain_parts = jnp.pad(jnp.stack([gain_one_part, gain_two_part], axis=1), ((0, 0), (0, 126)))
    kv_part = jnp.concatenate([across_tokens(normed, lin_kv), gain_parts], axis=1).astype(low)
    kv_sum = lax.psum_scatter(kv_part, "rows", scatter_dimension=0, tiled=True)
    attn_sum = jnp.concatenate([query_sum, kv_sum], axis=1)
    attn_grad = ring_reduce(attn_sum.reshape(seq_count, -1, attn_sum.shape[1]), "seq")
    end = q_cols + 2 * kv_cols
    return (
        layer_out[None],
        input_grad[None],
        attn_grad[:, end],
        attn_grad[:, :q_cols],
        attn_grad[:, q_cols : q_cols + kv_cols],
        attn_grad[:, q_cols + kv_cols : end],
        out_grad,
        attn_grad[:, end + 1],
        gate_grad,
        up_grad,
        down_grad,
    )


def solution(mesh):
    placed = (
        P("rows", "seq", None),
        P("rows", "seq", None),
        P("rows", None),
        P(("rows", "seq")),
        P(("rows", "seq"), None),
        P(("rows", "seq"), None),
        P(("rows", "seq"), None),
        P(("rows", "seq"), None),
        P(("rows", "seq")),
        P(("rows", "seq"), None),
        P(("rows", "seq"), None),
        P(("rows", "seq"), None),
    )
    return jax.shard_map(
        local,
        mesh=mesh,
        in_specs=placed,
        out_specs=(
            P("rows", "seq", None),
            P("rows", "seq", None),
            P(("rows", "seq")),
            P(("rows", "seq"), None),
            P(("rows", "seq"), None),
            P(("rows", "seq"), None),
            P(("rows", "seq"), None),
            P(("rows", "seq")),
            P(("rows", "seq"), None),
            P(("rows", "seq"), None),
            P(("rows", "seq"), None),
        ),
        check_vma=False,
    )
```

```python
import functools
import math

import jax
import jax.numpy as jnp
from jax import lax
from jax.experimental import pallas as pl
from jax.experimental.pallas import tpu as pltpu
from jax.sharding import PartitionSpec as P

HEAD_DIM = 64
HALF = HEAD_DIM // 2
PAIR = 2 * HEAD_DIM
MEMBERS = 2


epsilon = 1e-05
rope_theta = 500000.0


def rope_table(head_width):
    listed = []
    for column in range(head_width // 2):
        natural = rope_theta ** (-2.0 * column / head_width)
        wavelength = 2.0 * math.pi / natural
        if wavelength > 8192.0:
            scaled = natural / 32.0
        elif wavelength < 2048.0:
            scaled = natural
        else:
            blending = (8192.0 / wavelength - 1.0) / 3.0
            scaled = (1.0 - blending) * natural / 32.0 + blending * natural
        listed.append(scaled)
    return jnp.asarray(listed + listed, dtype=jnp.float32)


def rms_scale(values):
    return lax.rsqrt(jnp.mean(values * values, axis=-1, keepdims=True) + epsilon)


def dense_low(left_side, right_side):
    return jnp.dot(left_side, right_side, preferred_element_type=jnp.float32)


def against_rows(left_side, right_side):
    return lax.dot_general(
        left_side, right_side, (((1,), (1,)), ((), ())), preferred_element_type=jnp.float32
    )


def across_tokens(left_side, right_side):
    return lax.dot_general(
        left_side, right_side, (((0,), (0,)), ((), ())), preferred_element_type=jnp.float32
    )


def norm_back(grad_normed, normed_unit, scale_rows, gain_full):
    scaled_grad = grad_normed * gain_full
    return scale_rows * (
        scaled_grad - normed_unit * jnp.mean(scaled_grad * normed_unit, axis=-1, keepdims=True)
    )


def tie(value, *others):
    return lax.optimization_barrier((value,) + others)[0]


def hop(block, axis, ahead=1):
    count = lax.axis_size(axis)
    return lax.ppermute(block, axis, [(i, (i + ahead) % count) for i in range(count)])


def ring_blocks(own, axis):
    blocks = [own]
    for _ in range(1, lax.axis_size(axis)):
        blocks.append(hop(blocks[-1], axis))
    return blocks


def direct_blocks(own, axis):
    return [own] + [hop(own, axis, ahead) for ahead in range(1, lax.axis_size(axis))]


def exchange(parts, axis):
    count = lax.axis_size(axis)
    here = lax.axis_index(axis)

    def block(ahead):
        return lax.dynamic_index_in_dim(parts, (here + ahead) % count, 0, keepdims=False)

    return [block(0)] + [hop(block(ahead), axis, ahead) for ahead in range(1, count)]


def in_order(blocks, axis):
    count = lax.axis_size(axis)
    here = lax.axis_index(axis)
    out = jnp.zeros((count,) + blocks[0].shape, blocks[0].dtype)
    for back, block in enumerate(blocks):
        out = lax.dynamic_update_index_in_dim(out, block, (here - back + count) % count, 0)
    return out


def sum_wide(blocks):
    return sum((block.astype(jnp.float32) for block in blocks[1:]), blocks[0].astype(jnp.float32))


def dot_of(left, right, left_dim, right_dim):
    return lax.dot_general(
        left, right, (((left_dim,), (right_dim,)), ((), ())), preferred_element_type=jnp.float32
    )


def in_half(block, upper):
    empty = jnp.zeros_like(block)
    return jnp.concatenate([empty, block] if upper else [block, empty], axis=0)


def make_bias(bias_ref, limits_ref):
    keys = lax.broadcasted_iota(jnp.int32, bias_ref.shape, 0)
    allowed = (keys <= limits_ref[0:1, :]) & (keys >= limits_ref[1:2, :])
    bias_ref[...] = jnp.where(allowed, 0.0, -1e30)


def rotated_queries(lin, cosine, sine):
    turned = lin.T
    heads = []
    for top in range(0, turned.shape[0], HEAD_DIM):
        upper, lower = turned[top : top + HALF], turned[top + HALF : top + HEAD_DIM]
        whole = jnp.concatenate(
            [upper * cosine[:HALF] - lower * sine[:HALF], lower * cosine[HALF:] + upper * sine[HALF:]],
            axis=0,
        )
        heads.append(whole.astype(jnp.bfloat16) * jnp.bfloat16(HEAD_DIM**-0.5))
    return heads


def attend_kernel(limits_ref, cos_ref, sin_ref, lin_ref, kv_ref, o_ref, lse_ref, bias_ref, ot_ref):
    @pl.when(pl.program_id(0) == 0)
    def _():
        make_bias(bias_ref, limits_ref)

    q_wide = lin_ref.shape[1] // MEMBERS
    group = q_wide // HEAD_DIM
    for member in range(MEMBERS):
        pair = kv_ref[:, :, member * PAIR : (member + 1) * PAIR].reshape(bias_ref.shape[0], PAIR)
        value = pair.T[HEAD_DIM:]
        lin = lin_ref[:, member * q_wide : (member + 1) * q_wide]
        queries = rotated_queries(lin, cos_ref[...], sin_ref[...])
        for index, query in enumerate(queries):
            head = member * group + index
            scores = dot_of(pair, in_half(query, False), 1, 0) + bias_ref[...]
            highest = jnp.max(scores, axis=0, keepdims=True)
            weights = jnp.exp(scores - highest)
            total = jnp.sum(weights, axis=0, keepdims=True)
            mixed = dot_of(value, weights.astype(jnp.bfloat16), 1, 0) / total
            ot_ref[head * HEAD_DIM : (head + 1) * HEAD_DIM, :] = mixed.astype(jnp.bfloat16)
            lse_ref[head : head + 1, :] = highest + jnp.log(total)
    o_ref[...] = ot_ref[...].T


def attend_back_kernel(
    limits_ref, cos_ref, sin_ref, lin_ref, kv_ref, do_ref, lse_ref,
    dq_ref, dq_heads_ref, dkv_ref, bias_ref, dqt_ref, acc_ref,
):
    @pl.when(pl.program_id(0) == 0)
    def _():
        make_bias(bias_ref, limits_ref)

    q_wide = lin_ref.shape[1] // MEMBERS
    group = q_wide // HEAD_DIM
    cosine, sine = cos_ref[...], sin_ref[...]
    for member in range(MEMBERS):
        lanes = slice(member * PAIR, (member + 1) * PAIR)
        pair = kv_ref[:, :, lanes].reshape(bias_ref.shape[0], PAIR)
        key = pair.T[:HEAD_DIM]
        lin = lin_ref[:, member * q_wide : (member + 1) * q_wide]
        queries = rotated_queries(lin, cosine, sine)
        grads = do_ref[:, member * q_wide : (member + 1) * q_wide].T
        for index, query in enumerate(queries):
            head = member * group + index
            rows = slice(index * HEAD_DIM, (index + 1) * HEAD_DIM)
            query = in_half(query, False)
            grad = in_half(grads[rows], True)
            scores = dot_of(pair, query, 1, 0) + bias_ref[...]
            weights = jnp.exp(scores - lse_ref[head : head + 1, :])
            grad_weights = dot_of(pair, grad, 1, 0)
            centre = jnp.sum(weights * grad_weights, axis=0, keepdims=True)
            grad_scores = (weights * (grad_weights - centre)).astype(jnp.bfloat16)
            back = (dot_of(key, grad_scores, 1, 0) * HEAD_DIM**-0.5).astype(jnp.bfloat16)
            back = back.astype(jnp.float32)
            upper, lower = back[:HALF], back[HALF:]
            dqt_ref[rows, :] = jnp.concatenate(
                [upper * cosine[:HALF] + lower * sine[:HALF],
                 lower * cosine[HALF:] - upper * sine[HALF:]], axis=0,
            ).astype(jnp.bfloat16)
            part = dot_of(grad_scores, query, 1, 1) + dot_of(
                weights.astype(jnp.bfloat16), grad, 1, 1
            )
            if index == 0:
                acc_ref[...] = part
            else:
                acc_ref[...] += part
        turned = dqt_ref[...].T
        dq_ref[:, member * q_wide : (member + 1) * q_wide] = turned
        dq_heads_ref[member] = turned
        dkv_ref[:, :, lanes] = acc_ref[...].astype(jnp.bfloat16).reshape(
            dkv_ref.shape[0], dkv_ref.shape[1], PAIR
        )


def attend_specs(lin, pairs):
    seq_count, tokens, kv_wide = pairs.shape
    kv_heads = kv_wide // PAIR
    q_wide = lin.shape[1] // kv_heads - PAIR
    return kv_heads, q_wide, (
        pl.BlockSpec((2, tokens), lambda i: (0, 0)),
        pl.BlockSpec((HEAD_DIM, tokens), lambda i: (0, 0)),
        pl.BlockSpec((seq_count, tokens, MEMBERS * PAIR), lambda i: (0, 0, i)),
        pl.BlockSpec((tokens, MEMBERS * q_wide), lambda i: (0, i)),
        pl.BlockSpec((MEMBERS * q_wide // HEAD_DIM, tokens), lambda i: (i, 0)),
        pl.BlockSpec((MEMBERS, tokens, q_wide), lambda i: (i, 0, 0)),
    )


def attend(lin, pairs, limits, cosine, sine):
    seq_count, tokens, _ = pairs.shape
    row_len = seq_count * tokens
    kv_heads, q_wide, (limit, table, pair, mixed, stats, _) = attend_specs(lin, pairs)
    q_cols = kv_heads * q_wide
    work = q_cols * tokens * row_len
    return pl.pallas_call(
        attend_kernel,
        grid=(kv_heads // MEMBERS,),
        in_specs=[limit, table, table, mixed, pair],
        out_specs=[mixed, stats],
        out_shape=[
            jax.ShapeDtypeStruct((tokens, q_cols), jnp.bfloat16),
            jax.ShapeDtypeStruct((q_cols // HEAD_DIM, tokens), jnp.float32),
        ],
        scratch_shapes=[
            pltpu.VMEM((row_len, tokens), jnp.float32),
            pltpu.VMEM((MEMBERS * q_wide, tokens), jnp.bfloat16),
        ],
        compiler_params=pltpu.CompilerParams(vmem_limit_bytes=40 * 1024 * 1024),
        cost_estimate=pl.CostEstimate(
            flops=48 * work, bytes_accessed=8 * 1024 * 1024, transcendentals=work // HEAD_DIM
        ),
        name="attend",
    )(limits, cosine, sine, lin, pairs)


def attend_back(lin, pairs, limits, cosine, sine, grads, log_totals):
    seq_count, tokens, _ = pairs.shape
    row_len = seq_count * tokens
    kv_heads, q_wide, (limit, table, pair, mixed, stats, back) = attend_specs(lin, pairs)
    work = kv_heads * q_wide * tokens * row_len
    return pl.pallas_call(
        attend_back_kernel,
        grid=(kv_heads // MEMBERS,),
        in_specs=[limit, table, table, mixed, pair, mixed, stats],
        out_specs=[mixed, back, pair],
        out_shape=[
            jax.ShapeDtypeStruct((tokens, kv_heads * q_wide), jnp.bfloat16),
            jax.ShapeDtypeStruct((kv_heads, tokens, q_wide), jnp.bfloat16),
            jax.ShapeDtypeStruct(pairs.shape, jnp.bfloat16),
        ],
        scratch_shapes=[
            pltpu.VMEM((row_len, tokens), jnp.float32),
            pltpu.VMEM((q_wide, tokens), jnp.bfloat16),
            pltpu.VMEM((row_len, PAIR), jnp.float32),
        ],
        compiler_params=pltpu.CompilerParams(vmem_limit_bytes=40 * 1024 * 1024),
        cost_estimate=pl.CostEstimate(
            flops=72 * work, bytes_accessed=12 * 1024 * 1024, transcendentals=work // HEAD_DIM
        ),
        name="attend_back",
    )(limits, cosine, sine, lin, pairs, grads, log_totals)


def from_heads(lin, count):
    heads, tokens, wide = lin.shape
    if count == heads:
        return lin
    lin = lin.reshape(heads, tokens, count // heads, -1)
    return jnp.transpose(lin, (0, 2, 1, 3)).reshape(count, tokens, -1)


def local(
    inputs,
    cotangent,
    doc_lengths,
    gain_attn,
    w_query,
    w_key,
    w_value,
    w_out,
    gain_mlp,
    w_gate,
    w_up,
    w_down,
):
    seq_count = lax.axis_size("seq")
    row_count = lax.axis_size("rows")
    local_len = inputs.shape[1]
    width = inputs.shape[2]
    row_len = local_len * seq_count
    q_cols, kv_cols = w_query.shape[1], w_key.shape[1]
    q_split, kv_split = q_cols // row_count, kv_cols // row_count
    kv_heads = kv_cols // HEAD_DIM
    slab_rows = w_query.shape[0]
    ff_local = w_gate.shape[1] // seq_count
    ff_block = w_down.shape[0]
    both = ("rows", "seq")
    low = jnp.bfloat16

    gains = jnp.stack([gain_attn, gain_mlp])
    gains = jnp.broadcast_to(gains[None], (row_count * seq_count,) + gains.shape)
    gains = lax.all_to_all(gains, both, split_axis=0, concat_axis=0, tiled=True)
    gains = jnp.transpose(gains, (1, 0, 2)).reshape(2, width).astype(jnp.float32)
    gain_one, gain_two = gains[0], gains[1]

    q_wide = q_cols // kv_heads
    kv_local = jnp.concatenate(
        [w_key.reshape(-1, kv_heads, HEAD_DIM), w_value.reshape(-1, kv_heads, HEAD_DIM)], axis=2
    ).reshape(slab_rows, -1)
    proj_seq = in_order(
        direct_blocks(jnp.concatenate([w_query, kv_local], axis=1), "seq"), "seq"
    )
    proj_full = lax.all_gather(
        proj_seq.reshape(seq_count * slab_rows, -1), "rows", axis=0, tiled=True
    )
    out_seq = in_order(direct_blocks(tie(w_out, proj_seq), "seq"), "seq")
    out_full = lax.all_gather(
        out_seq.reshape(seq_count * slab_rows, -1), "rows", axis=0, tiled=True
    )

    def slab_of(weight):
        cut = weight.reshape(slab_rows, row_count, seq_count, ff_block)
        return jnp.transpose(cut, (2, 0, 1, 3)).reshape(seq_count, slab_rows, ff_local)

    slab = jnp.concatenate([slab_of(w_gate), slab_of(w_up)], axis=2)
    slab = in_order(exchange(tie(slab, out_seq), "seq"), "seq")
    slab = slab.reshape(seq_count * slab_rows, 2 * ff_local)
    gate_up_full = lax.all_gather(slab, "rows", axis=0, tiled=True)

    places = jnp.arange(row_len, dtype=jnp.int32)
    row_lengths = doc_lengths[0]
    doc_ends = jnp.cumsum(row_lengths)
    doc_starts = doc_ends - row_lengths
    inside = (places[:, None] >= doc_starts[None, :]) & (places[:, None] < doc_ends[None, :])
    token_start = jnp.sum(jnp.where(inside, doc_starts[None, :], 0), axis=1)
    offset = lax.axis_index("seq") * local_len
    local_places = lax.dynamic_slice_in_dim(places, offset, local_len)
    local_start = lax.dynamic_slice_in_dim(token_start, offset, local_len)
    limits = jnp.stack([local_places, local_start])
    frequency = rope_table(HEAD_DIM)
    angles = (local_places - local_start).astype(jnp.float32)[:, None] * frequency[None, :]
    cosine, sine = jnp.cos(angles), jnp.sin(angles)
    cosine_t, sine_t = cosine.T, sine.T

    def turn_keys(pair, sign):
        pair = pair.reshape(local_len, kv_heads, PAIR)
        upper, lower, rest = pair[..., :HALF], pair[..., HALF:HEAD_DIM], pair[..., HEAD_DIM:]
        cos_half, sin_half = cosine[:, None, :HALF], sign * sine[:, None, :HALF]
        return jnp.concatenate(
            [upper * cos_half - lower * sin_half, lower * cos_half + upper * sin_half, rest], axis=-1
        )

    inputs_f = inputs[0].astype(jnp.float32)
    scale_one = rms_scale(inputs_f)
    unit_one = inputs_f * scale_one
    normed = (unit_one * gain_one).astype(low)
    lin = dense_low(normed, proj_full)
    pair_local = turn_keys(lin[:, q_cols:], 1.0).astype(low).reshape(local_len, -1)
    pairs = in_order(direct_blocks(pair_local, "seq"), "seq")
    down_full = lax.all_gather(tie(w_down, pairs), "rows", axis=0, tiled=True)
    grad_blocks = [cotangent[0], hop(tie(cotangent[0], pairs), "seq")]
    attended, log_totals = attend(lin, pairs, limits, cosine_t, sine_t)
    attended = tie(attended, grad_blocks[1])

    hidden_one = inputs_f + dense_low(attended, out_full)
    scale_two = rms_scale(hidden_one)
    unit_two = hidden_one * scale_two
    normed_two = (unit_two * gain_two).astype(low)
    normed_full = lax.all_gather(tie(normed, normed_two), "rows", axis=0, tiled=True)

    blocks = ring_blocks(normed_two, "seq")
    for step in range(2, seq_count):
        grad_blocks.append(hop(tie(grad_blocks[-1], blocks[-1]), "seq"))
    tokens = jnp.concatenate(blocks)
    gate_up = dense_low(tokens, gate_up_full)
    grad_tokens = jnp.concatenate(grad_blocks)
    grad_inner = against_rows(tie(grad_tokens, gate_up), down_full)
    gate_value, up_value = gate_up[:, :ff_local], gate_up[:, ff_local:]
    sigmoid_gate = jax.nn.sigmoid(gate_value)
    inner_act = (gate_value * sigmoid_gate * up_value).astype(low)
    grad_up = (grad_inner * gate_value * sigmoid_gate).astype(low)
    grad_gate = (
        grad_inner * up_value * sigmoid_gate * (1.0 + gate_value * (1.0 - sigmoid_gate))
    ).astype(low)
    grad_pair = jnp.concatenate([grad_gate, grad_up], axis=1)
    back = against_rows(grad_pair, gate_up_full).astype(low)

    def block_of(whole, step):
        start = (step % seq_count) * local_len
        return whole[start : start + local_len]

    total = block_of(back, 1)
    for step in range(1, seq_count):
        arrived = hop(total, "seq")
        if step == 1:
            gate_up_part = across_tokens(tie(tokens, back), grad_pair).astype(low)
            arrived = tie(arrived, gate_up_part)
        if step == 2:
            down_part = across_tokens(tie(inner_act, total), grad_tokens).astype(low)
            mixed_part = dense_low(tie(inner_act, down_part), down_full).astype(low)
            arrived = tie(arrived, mixed_part)
        total = arrived.astype(jnp.float32) + block_of(back, step + 1).astype(jnp.float32)
        if step < seq_count - 1:
            total = total.astype(low)
    grad_normed_two = total
    mixed = hop(tie(block_of(mixed_part, 1), grad_normed_two), "seq")
    gate_up_sum = lax.psum_scatter(gate_up_part, "rows", scatter_dimension=0, tiled=True)
    grad_out = cotangent[0].astype(jnp.float32)
    gain_two_part = jnp.sum(grad_normed_two * unit_two, axis=0)
    grad_hidden = grad_out + norm_back(grad_normed_two, unit_two, scale_two, gain_two)
    grad_branch = grad_hidden.astype(low)
    grad_attended = against_rows(grad_branch, out_full).astype(low)

    back_q, back_heads, pair_part = attend_back(
        lin, pairs, limits, cosine_t, sine_t, grad_attended, log_totals
    )
    back_q, back_heads, pair_part = tie((back_q, back_heads, pair_part), mixed, gate_up_sum)
    out_part = across_tokens(tie(attended, pair_part), grad_branch).astype(low)
    out_sum = lax.psum_scatter(out_part, "rows", scatter_dimension=0, tiled=True)
    down_grad = lax.psum_scatter(
        tie(down_part, out_part), "rows", scatter_dimension=0, tiled=True
    )
    pair_grad = sum_wide(exchange(pair_part, "seq")).astype(low)
    back_kv = turn_keys(pair_grad.astype(jnp.float32), -1.0).astype(low)
    kv_heads_first = jnp.transpose(back_kv, (1, 0, 2))
    if row_count == kv_heads:
        lin_back = jnp.concatenate([back_heads, kv_heads_first], axis=2)
    else:
        lin_back = jnp.concatenate(
            [from_heads(back_heads, row_count),
             from_heads(kv_heads_first[:, :, :HEAD_DIM], row_count),
             from_heads(kv_heads_first[:, :, HEAD_DIM:], row_count)], axis=2
        )
    mine = lax.all_to_all(lin_back, "rows", split_axis=0, concat_axis=0, tiled=True)
    part = across_tokens(normed_full, mine.reshape(-1, mine.shape[-1])).astype(low)
    gate_up_blocks = exchange(
        tie(gate_up_sum, pair_grad).reshape(seq_count, slab_rows, 2 * ff_local), "seq"
    )
    mixed = mixed.astype(jnp.float32) + block_of(mixed_part, 2).astype(jnp.float32)
    for step in range(2, seq_count):
        mixed = hop(tie(mixed.astype(low), pair_grad), "seq")
        if step == 2:
            part = tie(part, mixed)
        mixed = mixed.astype(jnp.float32) + block_of(mixed_part, step + 1).astype(jnp.float32)
    part = part.reshape(row_count * seq_count, slab_rows, -1)
    part = lax.all_to_all(part, both, split_axis=0, concat_axis=0, tiled=True)
    part = part.reshape(row_count, seq_count, slab_rows, -1).astype(jnp.float32)
    proj_grad = jnp.transpose(jnp.sum(part, axis=1), (1, 0, 2))
    query_grad = proj_grad[:, :, :q_split].reshape(-1, q_cols)
    key_grad = proj_grad[:, :, q_split : q_split + kv_split].reshape(-1, kv_cols)
    value_grad = proj_grad[:, :, q_split + kv_split :].reshape(-1, kv_cols)
    layer_out = (hidden_one + mixed).astype(low)
    out_grad = sum_wide(exchange(out_sum.reshape(seq_count, -1, width), "seq"))
    grad_normed = against_rows(
        jnp.concatenate([back_q, back_kv.reshape(local_len, -1)], axis=1), proj_full
    )
    gain_one_part = jnp.sum(grad_normed * unit_one, axis=0)
    input_grad = (
        grad_hidden + norm_back(grad_normed, unit_one, scale_one, gain_one)
    ).astype(low)
    gain_parts = jnp.stack([gain_one_part, gain_two_part], axis=0)
    gain_parts = jnp.transpose(
        gain_parts.reshape(2, row_count * seq_count, -1), (1, 0, 2)
    )
    gain_sums = jnp.sum(
        lax.all_to_all(gain_parts, both, split_axis=0, concat_axis=0, tiled=True), axis=0
    )
    gate_up_back = in_order(gate_up_blocks, "seq").astype(jnp.float32)
    gate_up_back = gate_up_back.reshape(seq_count, slab_rows, 2, row_count, ff_block)
    gate_up_back = jnp.transpose(gate_up_back, (2, 1, 3, 0, 4))
    gate_grad = gate_up_back[0].reshape(slab_rows, -1)
    up_grad = gate_up_back[1].reshape(slab_rows, -1)
    down_grad = tie(down_grad, input_grad).astype(jnp.float32)
    return (
        layer_out[None],
        input_grad[None],
        gain_sums[0],
        query_grad,
        key_grad,
        value_grad,
        out_grad,
        gain_sums[1],
        gate_grad,
        up_grad,
        down_grad,
    )


def solution(mesh):
    placed = (
        P("rows", "seq", None),
        P("rows", "seq", None),
        P("rows", None),
        P(("rows", "seq")),
        P(("rows", "seq"), None),
        P(("rows", "seq"), None),
        P(("rows", "seq"), None),
        P(("rows", "seq"), None),
        P(("rows", "seq")),
        P(("rows", "seq"), None),
        P(("rows", "seq"), None),
        P(("rows", "seq"), None),
    )
    return jax.shard_map(
        local,
        mesh=mesh,
        in_specs=placed,
        out_specs=(
            P("rows", "seq", None),
            P("rows", "seq", None),
            P(("rows", "seq")),
            P(("rows", "seq"), None),
            P(("rows", "seq"), None),
            P(("rows", "seq"), None),
            P(("rows", "seq"), None),
            P(("rows", "seq")),
            P(("rows", "seq"), None),
            P(("rows", "seq"), None),
            P(("rows", "seq"), None),
        ),
        check_vma=False,
    )
```

```python
import functools
import math

import jax
import jax.numpy as jnp
from jax import lax
from jax.experimental import pallas as pl
from jax.experimental.pallas import tpu as pltpu
from jax.sharding import PartitionSpec as P

HEAD_DIM = 64
HALF = HEAD_DIM // 2
PAIR = 2 * HEAD_DIM
MEMBERS = 2


epsilon = 1e-05
rope_theta = 500000.0


def rope_table(head_width):
    listed = []
    for column in range(head_width // 2):
        natural = rope_theta ** (-2.0 * column / head_width)
        wavelength = 2.0 * math.pi / natural
        if wavelength > 8192.0:
            scaled = natural / 32.0
        elif wavelength < 2048.0:
            scaled = natural
        else:
            blending = (8192.0 / wavelength - 1.0) / 3.0
            scaled = (1.0 - blending) * natural / 32.0 + blending * natural
        listed.append(scaled)
    return jnp.asarray(listed + listed, dtype=jnp.float32)


def rms_scale(values):
    return lax.rsqrt(jnp.mean(values * values, axis=-1, keepdims=True) + epsilon)


def dense_low(left_side, right_side):
    return jnp.dot(left_side, right_side, preferred_element_type=jnp.float32)


def against_rows(left_side, right_side):
    return lax.dot_general(
        left_side, right_side, (((1,), (1,)), ((), ())), preferred_element_type=jnp.float32
    )


def across_tokens(left_side, right_side):
    return lax.dot_general(
        left_side, right_side, (((0,), (0,)), ((), ())), preferred_element_type=jnp.float32
    )


def norm_back(grad_normed, normed_unit, scale_rows, gain_full):
    scaled_grad = grad_normed * gain_full
    return scale_rows * (
        scaled_grad - normed_unit * jnp.mean(scaled_grad * normed_unit, axis=-1, keepdims=True)
    )


def tie(value, *others):
    return lax.optimization_barrier((value,) + others)[0]


def hop(block, axis, ahead=1):
    count = lax.axis_size(axis)
    return lax.ppermute(block, axis, [(i, (i + ahead) % count) for i in range(count)])


def ring_blocks(own, axis):
    blocks = [own]
    for _ in range(1, lax.axis_size(axis)):
        blocks.append(hop(blocks[-1], axis))
    return blocks


def direct_blocks(own, axis):
    return [own] + [hop(own, axis, ahead) for ahead in range(1, lax.axis_size(axis))]


def exchange(parts, axis):
    count = lax.axis_size(axis)
    here = lax.axis_index(axis)

    def block(ahead):
        return lax.dynamic_index_in_dim(parts, (here + ahead) % count, 0, keepdims=False)

    return [block(0)] + [hop(block(ahead), axis, ahead) for ahead in range(1, count)]


def in_order(blocks, axis):
    count = lax.axis_size(axis)
    here = lax.axis_index(axis)
    out = jnp.zeros((count,) + blocks[0].shape, blocks[0].dtype)
    for back, block in enumerate(blocks):
        out = lax.dynamic_update_index_in_dim(out, block, (here - back + count) % count, 0)
    return out


def sum_wide(blocks):
    return sum((block.astype(jnp.float32) for block in blocks[1:]), blocks[0].astype(jnp.float32))


def dot_of(left, right, left_dim, right_dim):
    return lax.dot_general(
        left, right, (((left_dim,), (right_dim,)), ((), ())), preferred_element_type=jnp.float32
    )


def in_half(block, upper):
    empty = jnp.zeros_like(block)
    return jnp.concatenate([empty, block] if upper else [block, empty], axis=0)


def make_bias(bias_ref, limits_ref):
    keys = lax.broadcasted_iota(jnp.int32, bias_ref.shape, 0)
    allowed = (keys <= limits_ref[0:1, :]) & (keys >= limits_ref[1:2, :])
    bias_ref[...] = jnp.where(allowed, 0.0, -1e30)


def rotated_queries(lin, cosine, sine):
    turned = lin.T
    heads = []
    for top in range(0, turned.shape[0], HEAD_DIM):
        upper, lower = turned[top : top + HALF], turned[top + HALF : top + HEAD_DIM]
        whole = jnp.concatenate(
            [upper * cosine[:HALF] - lower * sine[:HALF], lower * cosine[HALF:] + upper * sine[HALF:]],
            axis=0,
        )
        heads.append(whole.astype(jnp.bfloat16) * jnp.bfloat16(HEAD_DIM**-0.5))
    return heads


def attend_kernel(limits_ref, cos_ref, sin_ref, lin_ref, kv_ref, o_ref, lse_ref, bias_ref, ot_ref):
    @pl.when(pl.program_id(0) == 0)
    def _():
        make_bias(bias_ref, limits_ref)

    q_wide = lin_ref.shape[1] // MEMBERS
    group = q_wide // HEAD_DIM
    for member in range(MEMBERS):
        pair = kv_ref[:, :, member * PAIR : (member + 1) * PAIR].reshape(bias_ref.shape[0], PAIR)
        value = pair.T[HEAD_DIM:]
        lin = lin_ref[:, member * q_wide : (member + 1) * q_wide]
        queries = rotated_queries(lin, cos_ref[...], sin_ref[...])
        for index, query in enumerate(queries):
            head = member * group + index
            scores = dot_of(pair, in_half(query, False), 1, 0) + bias_ref[...]
            highest = jnp.max(scores, axis=0, keepdims=True)
            weights = jnp.exp(scores - highest)
            total = jnp.sum(weights, axis=0, keepdims=True)
            mixed = dot_of(value, weights.astype(jnp.bfloat16), 1, 0) / total
            ot_ref[head * HEAD_DIM : (head + 1) * HEAD_DIM, :] = mixed.astype(jnp.bfloat16)
            lse_ref[head : head + 1, :] = highest + jnp.log(total)
    o_ref[...] = ot_ref[...].T


def attend_back_kernel(
    limits_ref, cos_ref, sin_ref, lin_ref, kv_ref, do_ref, lse_ref,
    dq_ref, dq_heads_ref, dkv_ref, bias_ref, dqt_ref, acc_ref,
):
    @pl.when(pl.program_id(0) == 0)
    def _():
        make_bias(bias_ref, limits_ref)

    q_wide = lin_ref.shape[1] // MEMBERS
    group = q_wide // HEAD_DIM
    cosine, sine = cos_ref[...], sin_ref[...]
    for member in range(MEMBERS):
        lanes = slice(member * PAIR, (member + 1) * PAIR)
        pair = kv_ref[:, :, lanes].reshape(bias_ref.shape[0], PAIR)
        key = pair.T[:HEAD_DIM]
        lin = lin_ref[:, member * q_wide : (member + 1) * q_wide]
        queries = rotated_queries(lin, cosine, sine)
        grads = do_ref[:, member * q_wide : (member + 1) * q_wide].T
        for index, query in enumerate(queries):
            head = member * group + index
            rows = slice(index * HEAD_DIM, (index + 1) * HEAD_DIM)
            query = in_half(query, False)
            grad = in_half(grads[rows], True)
            scores = dot_of(pair, query, 1, 0) + bias_ref[...]
            weights = jnp.exp(scores - lse_ref[head : head + 1, :])
            grad_weights = dot_of(pair, grad, 1, 0)
            centre = jnp.sum(weights * grad_weights, axis=0, keepdims=True)
            grad_scores = (weights * (grad_weights - centre)).astype(jnp.bfloat16)
            back = (dot_of(key, grad_scores, 1, 0) * HEAD_DIM**-0.5).astype(jnp.bfloat16)
            back = back.astype(jnp.float32)
            upper, lower = back[:HALF], back[HALF:]
            dqt_ref[rows, :] = jnp.concatenate(
                [upper * cosine[:HALF] + lower * sine[:HALF],
                 lower * cosine[HALF:] - upper * sine[HALF:]], axis=0,
            ).astype(jnp.bfloat16)
            part = dot_of(grad_scores, query, 1, 1) + dot_of(
                weights.astype(jnp.bfloat16), grad, 1, 1
            )
            if index == 0:
                acc_ref[...] = part
            else:
                acc_ref[...] += part
        turned = dqt_ref[...].T
        dq_ref[:, member * q_wide : (member + 1) * q_wide] = turned
        dq_heads_ref[member] = turned
        dkv_ref[:, :, lanes] = acc_ref[...].astype(jnp.bfloat16).reshape(
            dkv_ref.shape[0], dkv_ref.shape[1], PAIR
        )


def attend_specs(lin, pairs):
    seq_count, tokens, kv_wide = pairs.shape
    kv_heads = kv_wide // PAIR
    q_wide = lin.shape[1] // kv_heads - PAIR
    return kv_heads, q_wide, (
        pl.BlockSpec((2, tokens), lambda i: (0, 0)),
        pl.BlockSpec((HEAD_DIM, tokens), lambda i: (0, 0)),
        pl.BlockSpec((seq_count, tokens, MEMBERS * PAIR), lambda i: (0, 0, i)),
        pl.BlockSpec((tokens, MEMBERS * q_wide), lambda i: (0, i)),
        pl.BlockSpec((MEMBERS * q_wide // HEAD_DIM, tokens), lambda i: (i, 0)),
        pl.BlockSpec((MEMBERS, tokens, q_wide), lambda i: (i, 0, 0)),
    )


def attend(lin, pairs, limits, cosine, sine):
    seq_count, tokens, _ = pairs.shape
    row_len = seq_count * tokens
    kv_heads, q_wide, (limit, table, pair, mixed, stats, _) = attend_specs(lin, pairs)
    q_cols = kv_heads * q_wide
    work = q_cols * tokens * row_len
    return pl.pallas_call(
        attend_kernel,
        grid=(kv_heads // MEMBERS,),
        in_specs=[limit, table, table, mixed, pair],
        out_specs=[mixed, stats],
        out_shape=[
            jax.ShapeDtypeStruct((tokens, q_cols), jnp.bfloat16),
            jax.ShapeDtypeStruct((q_cols // HEAD_DIM, tokens), jnp.float32),
        ],
        scratch_shapes=[
            pltpu.VMEM((row_len, tokens), jnp.float32),
            pltpu.VMEM((MEMBERS * q_wide, tokens), jnp.bfloat16),
        ],
        compiler_params=pltpu.CompilerParams(vmem_limit_bytes=40 * 1024 * 1024),
        cost_estimate=pl.CostEstimate(
            flops=48 * work, bytes_accessed=8 * 1024 * 1024, transcendentals=work // HEAD_DIM
        ),
        name="attend",
    )(limits, cosine, sine, lin, pairs)


def attend_back(lin, pairs, limits, cosine, sine, grads, log_totals):
    seq_count, tokens, _ = pairs.shape
    row_len = seq_count * tokens
    kv_heads, q_wide, (limit, table, pair, mixed, stats, back) = attend_specs(lin, pairs)
    work = kv_heads * q_wide * tokens * row_len
    return pl.pallas_call(
        attend_back_kernel,
        grid=(kv_heads // MEMBERS,),
        in_specs=[limit, table, table, mixed, pair, mixed, stats],
        out_specs=[mixed, back, pair],
        out_shape=[
            jax.ShapeDtypeStruct((tokens, kv_heads * q_wide), jnp.bfloat16),
            jax.ShapeDtypeStruct((kv_heads, tokens, q_wide), jnp.bfloat16),
            jax.ShapeDtypeStruct(pairs.shape, jnp.bfloat16),
        ],
        scratch_shapes=[
            pltpu.VMEM((row_len, tokens), jnp.float32),
            pltpu.VMEM((q_wide, tokens), jnp.bfloat16),
            pltpu.VMEM((row_len, PAIR), jnp.float32),
        ],
        compiler_params=pltpu.CompilerParams(vmem_limit_bytes=40 * 1024 * 1024),
        cost_estimate=pl.CostEstimate(
            flops=72 * work, bytes_accessed=12 * 1024 * 1024, transcendentals=work // HEAD_DIM
        ),
        name="attend_back",
    )(limits, cosine, sine, lin, pairs, grads, log_totals)


def from_heads(lin, count):
    heads, tokens, wide = lin.shape
    if count == heads:
        return lin
    lin = lin.reshape(heads, tokens, count // heads, -1)
    return jnp.transpose(lin, (0, 2, 1, 3)).reshape(count, tokens, -1)


def local(
    inputs,
    cotangent,
    doc_lengths,
    gain_attn,
    w_query,
    w_key,
    w_value,
    w_out,
    gain_mlp,
    w_gate,
    w_up,
    w_down,
):
    seq_count = lax.axis_size("seq")
    row_count = lax.axis_size("rows")
    local_len = inputs.shape[1]
    width = inputs.shape[2]
    row_len = local_len * seq_count
    q_cols, kv_cols = w_query.shape[1], w_key.shape[1]
    q_split, kv_split = q_cols // row_count, kv_cols // row_count
    kv_heads = kv_cols // HEAD_DIM
    slab_rows = w_query.shape[0]
    ff_local = w_gate.shape[1] // seq_count
    ff_block = w_down.shape[0]
    both = ("rows", "seq")
    low = jnp.bfloat16

    q_wide = q_cols // kv_heads
    kv_local = jnp.concatenate(
        [w_key.reshape(-1, kv_heads, HEAD_DIM), w_value.reshape(-1, kv_heads, HEAD_DIM)], axis=2
    ).reshape(slab_rows, -1)
    gains = jnp.pad(jnp.stack([gain_attn, gain_mlp], axis=1), ((0, 0), (0, 126)))
    proj_seq = in_order(
        direct_blocks(jnp.concatenate([w_query, kv_local, gains], axis=1), "seq"), "seq"
    )
    gathered = lax.all_gather(
        proj_seq.reshape(seq_count * slab_rows, -1), "rows", axis=0, tiled=True
    )
    proj_full = gathered[:, : q_cols + 2 * kv_cols]
    gains = gathered[:, q_cols + 2 * kv_cols :].T.astype(jnp.float32)
    gain_one, gain_two = gains[0], gains[1]
    out_seq = in_order(direct_blocks(tie(w_out, proj_seq), "seq"), "seq")
    out_full = lax.all_gather(
        out_seq.reshape(seq_count * slab_rows, -1), "rows", axis=0, tiled=True
    )

    def slab_of(weight):
        cut = weight.reshape(slab_rows, row_count, seq_count, ff_block)
        return jnp.transpose(cut, (2, 0, 1, 3)).reshape(seq_count, slab_rows, ff_local)

    slab = jnp.concatenate([slab_of(w_gate), slab_of(w_up)], axis=2)
    grad_blocks = [cotangent[0], hop(tie(cotangent[0], out_seq), "seq")]
    slab_blocks = exchange(tie(slab, grad_blocks[1]), "seq")

    places = jnp.arange(row_len, dtype=jnp.int32)
    row_lengths = doc_lengths[0]
    doc_ends = jnp.cumsum(row_lengths)
    doc_starts = doc_ends - row_lengths
    inside = (places[:, None] >= doc_starts[None, :]) & (places[:, None] < doc_ends[None, :])
    token_start = jnp.sum(jnp.where(inside, doc_starts[None, :], 0), axis=1)
    offset = lax.axis_index("seq") * local_len
    local_places = lax.dynamic_slice_in_dim(places, offset, local_len)
    local_start = lax.dynamic_slice_in_dim(token_start, offset, local_len)
    limits = jnp.stack([local_places, local_start])
    frequency = rope_table(HEAD_DIM)
    angles = (local_places - local_start).astype(jnp.float32)[:, None] * frequency[None, :]
    cosine, sine = jnp.cos(angles), jnp.sin(angles)
    cosine_t, sine_t = cosine.T, sine.T

    def turn_keys(pair, sign):
        pair = pair.reshape(local_len, kv_heads, PAIR)
        upper, lower, rest = pair[..., :HALF], pair[..., HALF:HEAD_DIM], pair[..., HEAD_DIM:]
        cos_half, sin_half = cosine[:, None, :HALF], sign * sine[:, None, :HALF]
        return jnp.concatenate(
            [upper * cos_half - lower * sin_half, lower * cos_half + upper * sin_half, rest], axis=-1
        )

    inputs_f = inputs[0].astype(jnp.float32)
    scale_one = rms_scale(inputs_f)
    unit_one = inputs_f * scale_one
    normed = (unit_one * gain_one).astype(low)
    lin = dense_low(normed, proj_full)
    pair_local = turn_keys(lin[:, q_cols:], 1.0).astype(low).reshape(local_len, -1)
    slab_blocks = tie(tuple(slab_blocks), pair_local)
    slab = in_order(slab_blocks, "seq").reshape(seq_count * slab_rows, 2 * ff_local)
    gate_up_full = lax.all_gather(slab, "rows", axis=0, tiled=True)
    pairs = in_order(direct_blocks(pair_local, "seq"), "seq")
    down_full = lax.all_gather(tie(w_down, pairs), "rows", axis=0, tiled=True)
    grad_blocks.append(hop(tie(grad_blocks[1], pairs), "seq"))
    attended, log_totals = attend(lin, pairs, limits, cosine_t, sine_t)
    attended = tie(attended, grad_blocks[2])

    hidden_one = inputs_f + dense_low(attended, out_full)
    scale_two = rms_scale(hidden_one)
    unit_two = hidden_one * scale_two
    normed_two = (unit_two * gain_two).astype(low)
    normed_full = lax.all_gather(tie(normed, normed_two), "rows", axis=0, tiled=True)

    middle = seq_count // 2
    blocks = [normed_two]
    for _ in range(1, middle):
        blocks.append(hop(blocks[-1], "seq"))
    tokens_a = jnp.concatenate(blocks)
    gate_up_a = dense_low(tokens_a, gate_up_full)
    blocks.append(hop(blocks[-1], "seq"))
    for step in range(middle + 1, seq_count):
        blocks.append(hop(tie(blocks[-1], gate_up_a) if step == middle + 1 else blocks[-1], "seq"))
    for _ in range(3, seq_count):
        grad_blocks.append(hop(tie(grad_blocks[-1], blocks[-1]), "seq"))
    tokens_b = jnp.concatenate(blocks[middle:])
    gate_up_b = dense_low(tokens_b, gate_up_full)

    def middle_grads(gate_up, grad_block):
        gate_value, up_value = gate_up[:, :ff_local], gate_up[:, ff_local:]
        sigmoid_gate = jax.nn.sigmoid(gate_value)
        act = (gate_value * sigmoid_gate * up_value).astype(low)
        grad_inner = against_rows(grad_block, down_full)
        grad_up = (grad_inner * gate_value * sigmoid_gate).astype(low)
        grad_gate = (
            grad_inner * up_value * sigmoid_gate * (1.0 + gate_value * (1.0 - sigmoid_gate))
        ).astype(low)
        grad_pair = jnp.concatenate([grad_gate, grad_up], axis=1)
        return act, grad_gate, grad_up, against_rows(grad_pair, gate_up_full).astype(low)

    def block_of(halves, step):
        half, place = divmod(step % seq_count, middle)
        return halves[half][place * local_len : (place + 1) * local_len]

    grads_a = jnp.concatenate(grad_blocks[:middle])
    grads_b = jnp.concatenate(grad_blocks[middle:])
    act_a, gate_a, up_a, back_a = middle_grads(gate_up_a, tie(grads_a, gate_up_b))
    total = block_of((back_a,), 1)
    for step in range(1, seq_count):
        arrived = hop(total, "seq")
        if step == 1:
            act_b, gate_b, up_b, back_b = middle_grads(gate_up_b, tie(grads_b, back_a))
            arrived = tie(arrived, back_b)
        if step == 2:
            tokens = tie(jnp.concatenate([tokens_a, tokens_b]), total, normed_full)
            gate_part = across_tokens(tokens, jnp.concatenate([gate_a, gate_b])).astype(low)
            up_part = across_tokens(
                tie(tokens, gate_part), jnp.concatenate([up_a, up_b])
            ).astype(low)
            arrived = tie(arrived, up_part)
        if step == 3:
            inner_act = jnp.concatenate([act_a, act_b])
            down_part = across_tokens(
                tie(inner_act, total), jnp.concatenate([grads_a, grads_b])
            ).astype(low)
            mixed_part = dense_low(tie(inner_act, down_part), down_full).astype(low)
            arrived = tie(arrived, mixed_part)
        total = arrived.astype(jnp.float32) + block_of((back_a, back_b), step + 1).astype(
            jnp.float32
        )
        if step < seq_count - 1:
            total = total.astype(low)
    mixed_halves = (mixed_part[: middle * local_len], mixed_part[middle * local_len :])
    grad_normed_two = total
    mixed = hop(tie(block_of(mixed_halves, 1), arrived), "seq")
    gate_sum = lax.psum_scatter(gate_part, "rows", scatter_dimension=0, tiled=True)
    up_sum = lax.psum_scatter(tie(up_part, gate_part), "rows", scatter_dimension=0, tiled=True)
    grad_out = cotangent[0].astype(jnp.float32)
    gain_two_part = jnp.sum(grad_normed_two * unit_two, axis=0)
    grad_hidden = grad_out + norm_back(grad_normed_two, unit_two, scale_two, gain_two)
    grad_branch = grad_hidden.astype(low)
    grad_attended = against_rows(grad_branch, out_full).astype(low)
    grad_attended = tie(grad_attended, gate_sum)
    gate_blocks = exchange(gate_sum.reshape(seq_count, slab_rows, ff_local), "seq")

    back_q, back_heads, pair_part = attend_back(
        lin, pairs, limits, cosine_t, sine_t, grad_attended, log_totals
    )
    back_q, back_heads, pair_part = tie(
        (back_q, back_heads, pair_part), mixed, *gate_blocks[1:]
    )
    pair_blocks = exchange(pair_part, "seq")
    out_part = across_tokens(tie(attended, pair_blocks[1]), grad_branch).astype(low)
    out_sum = lax.psum_scatter(out_part, "rows", scatter_dimension=0, tiled=True)
    down_grad = lax.psum_scatter(
        tie(down_part, out_part), "rows", scatter_dimension=0, tiled=True
    )
    pair_grad = sum_wide(pair_blocks).astype(low)
    back_kv = turn_keys(pair_grad.astype(jnp.float32), -1.0).astype(low)
    kv_heads_first = jnp.transpose(back_kv, (1, 0, 2))
    if row_count == kv_heads:
        lin_back = jnp.concatenate([back_heads, kv_heads_first], axis=2)
    else:
        lin_back = jnp.concatenate(
            [from_heads(back_heads, row_count),
             from_heads(kv_heads_first[:, :, :HEAD_DIM], row_count),
             from_heads(kv_heads_first[:, :, HEAD_DIM:], row_count)], axis=2
        )
    mine = lax.all_to_all(lin_back, "rows", split_axis=0, concat_axis=0, tiled=True)
    mixed = mixed.astype(jnp.float32) + block_of(mixed_halves, 2).astype(jnp.float32)
    mixed = hop(tie(mixed.astype(low), lin_back), "seq")
    up_blocks = exchange(tie(up_sum, lin_back).reshape(seq_count, slab_rows, ff_local), "seq")
    part = across_tokens(normed_full, mine.reshape(-1, mine.shape[-1])).astype(low)
    part = part.reshape(row_count * seq_count, slab_rows, -1)
    part = lax.all_to_all(part, both, split_axis=0, concat_axis=0, tiled=True)
    part_raw = part
    for step in range(3, seq_count):
        mixed = mixed.astype(jnp.float32) + block_of(mixed_halves, step).astype(jnp.float32)
        mixed = hop(tie(mixed.astype(low), part_raw), "seq")
    mixed = mixed.astype(jnp.float32) + block_of(mixed_halves, seq_count).astype(jnp.float32)
    part = part.reshape(row_count, seq_count, slab_rows, -1).astype(jnp.float32)
    proj_grad = jnp.transpose(jnp.sum(part, axis=1), (1, 0, 2))
    query_grad = proj_grad[:, :, :q_split].reshape(-1, q_cols)
    key_grad = proj_grad[:, :, q_split : q_split + kv_split].reshape(-1, kv_cols)
    value_grad = proj_grad[:, :, q_split + kv_split :].reshape(-1, kv_cols)
    layer_out = (hidden_one + mixed).astype(low)
    out_grad = sum_wide(exchange(out_sum.reshape(seq_count, -1, width), "seq"))
    grad_normed = against_rows(
        jnp.concatenate([back_q, back_kv.reshape(local_len, -1)], axis=1), proj_full
    )
    gain_one_part = jnp.sum(grad_normed * unit_one, axis=0)
    input_grad = (
        grad_hidden + norm_back(grad_normed, unit_one, scale_one, gain_one)
    ).astype(low)
    gain_parts = jnp.stack([gain_one_part, gain_two_part], axis=0)
    gain_parts = tie(gain_parts, part_raw)
    gain_parts = jnp.transpose(
        gain_parts.reshape(2, row_count * seq_count, -1), (1, 0, 2)
    )
    gain_sums = jnp.sum(
        lax.all_to_all(gain_parts, both, split_axis=0, concat_axis=0, tiled=True), axis=0
    )
    def owners_rows(blocks):
        whole = in_order(blocks, "seq").astype(jnp.float32)
        whole = whole.reshape(seq_count, slab_rows, row_count, ff_block)
        return jnp.transpose(whole, (1, 2, 0, 3)).reshape(slab_rows, -1)

    gate_grad = owners_rows(tie(tuple(gate_blocks), mine))
    up_grad = owners_rows(up_blocks)
    down_grad = tie(down_grad, input_grad).astype(jnp.float32)
    return (
        layer_out[None],
        input_grad[None],
        gain_sums[0],
        query_grad,
        key_grad,
        value_grad,
        out_grad,
        gain_sums[1],
        gate_grad,
        up_grad,
        down_grad,
    )


def solution(mesh):
    placed = (
        P("rows", "seq", None),
        P("rows", "seq", None),
        P("rows", None),
        P(("rows", "seq")),
        P(("rows", "seq"), None),
        P(("rows", "seq"), None),
        P(("rows", "seq"), None),
        P(("rows", "seq"), None),
        P(("rows", "seq")),
        P(("rows", "seq"), None),
        P(("rows", "seq"), None),
        P(("rows", "seq"), None),
    )
    return jax.shard_map(
        local,
        mesh=mesh,
        in_specs=placed,
        out_specs=(
            P("rows", "seq", None),
            P("rows", "seq", None),
            P(("rows", "seq")),
            P(("rows", "seq"), None),
            P(("rows", "seq"), None),
            P(("rows", "seq"), None),
            P(("rows", "seq"), None),
            P(("rows", "seq")),
            P(("rows", "seq"), None),
            P(("rows", "seq"), None),
            P(("rows", "seq"), None),
        ),
        check_vma=False,
    )
```

```python
import functools
import math

import jax
import jax.numpy as jnp
from jax import lax
from jax.experimental import pallas as pl
from jax.experimental.pallas import tpu as pltpu
from jax.sharding import PartitionSpec as P

HEAD_DIM = 64
HALF = HEAD_DIM // 2
PAIR = 2 * HEAD_DIM
MEMBERS = 2


epsilon = 1e-05
rope_theta = 500000.0


def rope_table(head_width):
    listed = []
    for column in range(head_width // 2):
        natural = rope_theta ** (-2.0 * column / head_width)
        wavelength = 2.0 * math.pi / natural
        if wavelength > 8192.0:
            scaled = natural / 32.0
        elif wavelength < 2048.0:
            scaled = natural
        else:
            blending = (8192.0 / wavelength - 1.0) / 3.0
            scaled = (1.0 - blending) * natural / 32.0 + blending * natural
        listed.append(scaled)
    return jnp.asarray(listed + listed, dtype=jnp.float32)


def rms_scale(values):
    return lax.rsqrt(jnp.mean(values * values, axis=-1, keepdims=True) + epsilon)


def dense_low(left_side, right_side):
    return jnp.dot(left_side, right_side, preferred_element_type=jnp.float32)


def against_rows(left_side, right_side):
    return lax.dot_general(
        left_side, right_side, (((1,), (1,)), ((), ())), preferred_element_type=jnp.float32
    )


def across_tokens(left_side, right_side):
    return lax.dot_general(
        left_side, right_side, (((0,), (0,)), ((), ())), preferred_element_type=jnp.float32
    )


def norm_back(grad_normed, normed_unit, scale_rows, gain_full):
    scaled_grad = grad_normed * gain_full
    return scale_rows * (
        scaled_grad - normed_unit * jnp.mean(scaled_grad * normed_unit, axis=-1, keepdims=True)
    )


def tie(value, *others):
    return lax.optimization_barrier((value,) + others)[0]


def hop(block, axis, ahead=1):
    count = lax.axis_size(axis)
    return lax.ppermute(block, axis, [(i, (i + ahead) % count) for i in range(count)])


def ring_blocks(own, axis):
    blocks = [own]
    for _ in range(1, lax.axis_size(axis)):
        blocks.append(hop(blocks[-1], axis))
    return blocks


def direct_blocks(own, axis):
    return [own] + [hop(own, axis, ahead) for ahead in range(1, lax.axis_size(axis))]


def exchange(parts, axis):
    count = lax.axis_size(axis)
    here = lax.axis_index(axis)

    def block(ahead):
        return lax.dynamic_index_in_dim(parts, (here + ahead) % count, 0, keepdims=False)

    return [block(0)] + [hop(block(ahead), axis, ahead) for ahead in range(1, count)]


def in_order(blocks, axis):
    count = lax.axis_size(axis)
    here = lax.axis_index(axis)
    out = jnp.zeros((count,) + blocks[0].shape, blocks[0].dtype)
    for back, block in enumerate(blocks):
        out = lax.dynamic_update_index_in_dim(out, block, (here - back + count) % count, 0)
    return out


def sum_wide(blocks):
    return sum((block.astype(jnp.float32) for block in blocks[1:]), blocks[0].astype(jnp.float32))


def dot_of(left, right, left_dim, right_dim):
    return lax.dot_general(
        left, right, (((left_dim,), (right_dim,)), ((), ())), preferred_element_type=jnp.float32
    )


def in_half(block, upper):
    empty = jnp.zeros_like(block)
    return jnp.concatenate([empty, block] if upper else [block, empty], axis=0)


def make_bias(bias_ref, limits_ref):
    keys = lax.broadcasted_iota(jnp.int32, bias_ref.shape, 0)
    allowed = (keys <= limits_ref[0:1, :]) & (keys >= limits_ref[1:2, :])
    bias_ref[...] = jnp.where(allowed, 0.0, -1e30)


def rotated_queries(lin, cosine, sine):
    turned = lin.T
    heads = []
    for top in range(0, turned.shape[0], HEAD_DIM):
        upper, lower = turned[top : top + HALF], turned[top + HALF : top + HEAD_DIM]
        whole = jnp.concatenate(
            [upper * cosine[:HALF] - lower * sine[:HALF], lower * cosine[HALF:] + upper * sine[HALF:]],
            axis=0,
        )
        heads.append(whole.astype(jnp.bfloat16) * jnp.bfloat16(HEAD_DIM**-0.5))
    return heads


def attend_kernel(limits_ref, cos_ref, sin_ref, lin_ref, kv_ref, o_ref, lse_ref, bias_ref, ot_ref):
    @pl.when(pl.program_id(0) == 0)
    def _():
        make_bias(bias_ref, limits_ref)

    q_wide = lin_ref.shape[1] // MEMBERS
    group = q_wide // HEAD_DIM
    for member in range(MEMBERS):
        pair = kv_ref[:, :, member * PAIR : (member + 1) * PAIR].reshape(bias_ref.shape[0], PAIR)
        value = pair.T[HEAD_DIM:]
        lin = lin_ref[:, member * q_wide : (member + 1) * q_wide]
        queries = rotated_queries(lin, cos_ref[...], sin_ref[...])
        for index, query in enumerate(queries):
            head = member * group + index
            scores = dot_of(pair, in_half(query, False), 1, 0) + bias_ref[...]
            highest = jnp.max(scores, axis=0, keepdims=True)
            weights = jnp.exp(scores - highest)
            total = jnp.sum(weights, axis=0, keepdims=True)
            mixed = dot_of(value, weights.astype(jnp.bfloat16), 1, 0) / total
            ot_ref[head * HEAD_DIM : (head + 1) * HEAD_DIM, :] = mixed.astype(jnp.bfloat16)
            lse_ref[head : head + 1, :] = highest + jnp.log(total)
    o_ref[...] = ot_ref[...].T


def attend_back_kernel(
    limits_ref, cos_ref, sin_ref, lin_ref, kv_ref, do_ref, lse_ref,
    dq_ref, dq_heads_ref, dkv_ref, bias_ref, dqt_ref, acc_ref,
):
    @pl.when(pl.program_id(0) == 0)
    def _():
        make_bias(bias_ref, limits_ref)

    q_wide = lin_ref.shape[1] // MEMBERS
    group = q_wide // HEAD_DIM
    cosine, sine = cos_ref[...], sin_ref[...]
    for member in range(MEMBERS):
        lanes = slice(member * PAIR, (member + 1) * PAIR)
        pair = kv_ref[:, :, lanes].reshape(bias_ref.shape[0], PAIR)
        key = pair.T[:HEAD_DIM]
        lin = lin_ref[:, member * q_wide : (member + 1) * q_wide]
        queries = rotated_queries(lin, cosine, sine)
        grads = do_ref[:, member * q_wide : (member + 1) * q_wide].T
        for index, query in enumerate(queries):
            head = member * group + index
            rows = slice(index * HEAD_DIM, (index + 1) * HEAD_DIM)
            query = in_half(query, False)
            grad = in_half(grads[rows], True)
            scores = dot_of(pair, query, 1, 0) + bias_ref[...]
            weights = jnp.exp(scores - lse_ref[head : head + 1, :])
            grad_weights = dot_of(pair, grad, 1, 0)
            centre = jnp.sum(weights * grad_weights, axis=0, keepdims=True)
            grad_scores = (weights * (grad_weights - centre)).astype(jnp.bfloat16)
            back = (dot_of(key, grad_scores, 1, 0) * HEAD_DIM**-0.5).astype(jnp.bfloat16)
            back = back.astype(jnp.float32)
            upper, lower = back[:HALF], back[HALF:]
            dqt_ref[rows, :] = jnp.concatenate(
                [upper * cosine[:HALF] + lower * sine[:HALF],
                 lower * cosine[HALF:] - upper * sine[HALF:]], axis=0,
            ).astype(jnp.bfloat16)
            part = dot_of(grad_scores, query, 1, 1) + dot_of(
                weights.astype(jnp.bfloat16), grad, 1, 1
            )
            if index == 0:
                acc_ref[...] = part
            else:
                acc_ref[...] += part
        turned = dqt_ref[...].T
        dq_ref[:, member * q_wide : (member + 1) * q_wide] = turned
        dq_heads_ref[member] = turned
        dkv_ref[:, :, lanes] = acc_ref[...].astype(jnp.bfloat16).reshape(
            dkv_ref.shape[0], dkv_ref.shape[1], PAIR
        )


def attend_specs(lin, pairs):
    seq_count, tokens, kv_wide = pairs.shape
    kv_heads = kv_wide // PAIR
    q_wide = lin.shape[1] // kv_heads - PAIR
    return kv_heads, q_wide, (
        pl.BlockSpec((2, tokens), lambda i: (0, 0)),
        pl.BlockSpec((HEAD_DIM, tokens), lambda i: (0, 0)),
        pl.BlockSpec((seq_count, tokens, MEMBERS * PAIR), lambda i: (0, 0, i)),
        pl.BlockSpec((tokens, MEMBERS * q_wide), lambda i: (0, i)),
        pl.BlockSpec((MEMBERS * q_wide // HEAD_DIM, tokens), lambda i: (i, 0)),
        pl.BlockSpec((MEMBERS, tokens, q_wide), lambda i: (i, 0, 0)),
    )


def attend(lin, pairs, limits, cosine, sine):
    seq_count, tokens, _ = pairs.shape
    row_len = seq_count * tokens
    kv_heads, q_wide, (limit, table, pair, mixed, stats, _) = attend_specs(lin, pairs)
    q_cols = kv_heads * q_wide
    work = q_cols * tokens * row_len
    return pl.pallas_call(
        attend_kernel,
        grid=(kv_heads // MEMBERS,),
        in_specs=[limit, table, table, mixed, pair],
        out_specs=[mixed, stats],
        out_shape=[
            jax.ShapeDtypeStruct((tokens, q_cols), jnp.bfloat16),
            jax.ShapeDtypeStruct((q_cols // HEAD_DIM, tokens), jnp.float32),
        ],
        scratch_shapes=[
            pltpu.VMEM((row_len, tokens), jnp.float32),
            pltpu.VMEM((MEMBERS * q_wide, tokens), jnp.bfloat16),
        ],
        compiler_params=pltpu.CompilerParams(vmem_limit_bytes=40 * 1024 * 1024),
        cost_estimate=pl.CostEstimate(
            flops=48 * work, bytes_accessed=8 * 1024 * 1024, transcendentals=work // HEAD_DIM
        ),
        name="attend",
    )(limits, cosine, sine, lin, pairs)


def attend_back(lin, pairs, limits, cosine, sine, grads, log_totals):
    seq_count, tokens, _ = pairs.shape
    row_len = seq_count * tokens
    kv_heads, q_wide, (limit, table, pair, mixed, stats, back) = attend_specs(lin, pairs)
    work = kv_heads * q_wide * tokens * row_len
    return pl.pallas_call(
        attend_back_kernel,
        grid=(kv_heads // MEMBERS,),
        in_specs=[limit, table, table, mixed, pair, mixed, stats],
        out_specs=[mixed, back, pair],
        out_shape=[
            jax.ShapeDtypeStruct((tokens, kv_heads * q_wide), jnp.bfloat16),
            jax.ShapeDtypeStruct((kv_heads, tokens, q_wide), jnp.bfloat16),
            jax.ShapeDtypeStruct(pairs.shape, jnp.bfloat16),
        ],
        scratch_shapes=[
            pltpu.VMEM((row_len, tokens), jnp.float32),
            pltpu.VMEM((q_wide, tokens), jnp.bfloat16),
            pltpu.VMEM((row_len, PAIR), jnp.float32),
        ],
        compiler_params=pltpu.CompilerParams(vmem_limit_bytes=40 * 1024 * 1024),
        cost_estimate=pl.CostEstimate(
            flops=72 * work, bytes_accessed=12 * 1024 * 1024, transcendentals=work // HEAD_DIM
        ),
        name="attend_back",
    )(limits, cosine, sine, lin, pairs, grads, log_totals)


def from_heads(lin, count):
    heads, tokens, wide = lin.shape
    if count == heads:
        return lin
    lin = lin.reshape(heads, tokens, count // heads, -1)
    return jnp.transpose(lin, (0, 2, 1, 3)).reshape(count, tokens, -1)


def local(
    inputs,
    cotangent,
    doc_lengths,
    gain_attn,
    w_query,
    w_key,
    w_value,
    w_out,
    gain_mlp,
    w_gate,
    w_up,
    w_down,
):
    seq_count = lax.axis_size("seq")
    row_count = lax.axis_size("rows")
    local_len = inputs.shape[1]
    width = inputs.shape[2]
    row_len = local_len * seq_count
    q_cols, kv_cols = w_query.shape[1], w_key.shape[1]
    q_split, kv_split = q_cols // row_count, kv_cols // row_count
    kv_heads = kv_cols // HEAD_DIM
    slab_rows = w_query.shape[0]
    ff_local = w_gate.shape[1] // seq_count
    ff_block = w_down.shape[0]
    both = ("rows", "seq")
    low = jnp.bfloat16

    q_wide = q_cols // kv_heads
    kv_local = jnp.concatenate(
        [w_key.reshape(-1, kv_heads, HEAD_DIM), w_value.reshape(-1, kv_heads, HEAD_DIM)], axis=2
    ).reshape(slab_rows, -1)
    gains = jnp.pad(jnp.stack([gain_attn, gain_mlp], axis=1), ((0, 0), (0, 126)))
    proj_seq = in_order(
        direct_blocks(jnp.concatenate([w_query, kv_local, gains], axis=1), "seq"), "seq"
    )
    gathered = lax.all_gather(
        proj_seq.reshape(seq_count * slab_rows, -1), "rows", axis=0, tiled=True
    )
    proj_full = gathered[:, : q_cols + 2 * kv_cols]
    gains = gathered[:, q_cols + 2 * kv_cols :].T.astype(jnp.float32)
    gain_one, gain_two = gains[0], gains[1]
    out_seq = in_order(direct_blocks(tie(w_out, proj_seq), "seq"), "seq")
    out_full = lax.all_gather(
        out_seq.reshape(seq_count * slab_rows, -1), "rows", axis=0, tiled=True
    )

    def slab_of(weight):
        cut = weight.reshape(slab_rows, row_count, seq_count, ff_block)
        return jnp.transpose(cut, (2, 0, 1, 3)).reshape(seq_count, slab_rows, ff_local)

    slab = jnp.concatenate([slab_of(w_gate), slab_of(w_up)], axis=2)
    grad_blocks = [cotangent[0], hop(tie(cotangent[0], out_seq), "seq")]
    slab_blocks = exchange(tie(slab, grad_blocks[1]), "seq")

    places = jnp.arange(row_len, dtype=jnp.int32)
    row_lengths = doc_lengths[0]
    doc_ends = jnp.cumsum(row_lengths)
    doc_starts = doc_ends - row_lengths
    inside = (places[:, None] >= doc_starts[None, :]) & (places[:, None] < doc_ends[None, :])
    token_start = jnp.sum(jnp.where(inside, doc_starts[None, :], 0), axis=1)
    offset = lax.axis_index("seq") * local_len
    local_places = lax.dynamic_slice_in_dim(places, offset, local_len)
    local_start = lax.dynamic_slice_in_dim(token_start, offset, local_len)
    limits = jnp.stack([local_places, local_start])
    frequency = rope_table(HEAD_DIM)
    angles = (local_places - local_start).astype(jnp.float32)[:, None] * frequency[None, :]
    cosine, sine = jnp.cos(angles), jnp.sin(angles)
    cosine_t, sine_t = cosine.T, sine.T

    def turn_keys(pair, sign):
        pair = pair.reshape(local_len, kv_heads, PAIR)
        upper, lower, rest = pair[..., :HALF], pair[..., HALF:HEAD_DIM], pair[..., HEAD_DIM:]
        cos_half, sin_half = cosine[:, None, :HALF], sign * sine[:, None, :HALF]
        return jnp.concatenate(
            [upper * cos_half - lower * sin_half, lower * cos_half + upper * sin_half, rest], axis=-1
        )

    inputs_f = inputs[0].astype(jnp.float32)
    scale_one = rms_scale(inputs_f)
    unit_one = inputs_f * scale_one
    normed = (unit_one * gain_one).astype(low)
    lin = dense_low(normed, proj_full)
    pair_local = turn_keys(lin[:, q_cols:], 1.0).astype(low).reshape(local_len, -1)
    slab_blocks = tie(tuple(slab_blocks), pair_local)
    slab = in_order(slab_blocks, "seq").reshape(seq_count * slab_rows, 2 * ff_local)
    gate_up_full = lax.all_gather(slab, "rows", axis=0, tiled=True)
    pairs = in_order(direct_blocks(pair_local, "seq"), "seq")
    down_full = lax.all_gather(tie(w_down, pairs), "rows", axis=0, tiled=True)
    grad_blocks.append(hop(tie(grad_blocks[1], pairs), "seq"))
    attended, log_totals = attend(lin, pairs, limits, cosine_t, sine_t)
    attended = tie(attended, grad_blocks[2])

    hidden_one = inputs_f + dense_low(attended, out_full)
    scale_two = rms_scale(hidden_one)
    unit_two = hidden_one * scale_two
    normed_two = (unit_two * gain_two).astype(low)
    normed_full = lax.all_gather(tie(normed, normed_two), "rows", axis=0, tiled=True)

    middle = seq_count // 2
    blocks = [normed_two]
    for _ in range(1, middle):
        blocks.append(hop(blocks[-1], "seq"))
    tokens_a = jnp.concatenate(blocks)
    gate_up_a = dense_low(tokens_a, gate_up_full)
    blocks.append(hop(blocks[-1], "seq"))
    for step in range(middle + 1, seq_count):
        blocks.append(hop(tie(blocks[-1], gate_up_a) if step == middle + 1 else blocks[-1], "seq"))
    for _ in range(3, seq_count):
        grad_blocks.append(hop(tie(grad_blocks[-1], blocks[-1]), "seq"))
    tokens_b = jnp.concatenate(blocks[middle:])
    gate_up_b = dense_low(tokens_b, gate_up_full)

    def middle_grads(gate_up, grad_block):
        gate_value, up_value = gate_up[:, :ff_local], gate_up[:, ff_local:]
        sigmoid_gate = jax.nn.sigmoid(gate_value)
        act = (gate_value * sigmoid_gate * up_value).astype(low)
        grad_inner = against_rows(grad_block, down_full)
        grad_up = (grad_inner * gate_value * sigmoid_gate).astype(low)
        grad_gate = (
            grad_inner * up_value * sigmoid_gate * (1.0 + gate_value * (1.0 - sigmoid_gate))
        ).astype(low)
        grad_pair = jnp.concatenate([grad_gate, grad_up], axis=1)
        return act, grad_gate, grad_up, against_rows(grad_pair, gate_up_full).astype(low)

    def block_of(halves, step):
        half, place = divmod(step % seq_count, middle)
        return halves[half][place * local_len : (place + 1) * local_len]

    grads_a = jnp.concatenate(grad_blocks[:middle])
    grads_b = jnp.concatenate(grad_blocks[middle:])
    act_a, gate_a, up_a, back_a = middle_grads(gate_up_a, tie(grads_a, gate_up_b))
    total = block_of((back_a,), 1)
    for step in range(1, seq_count):
        arrived = hop(total, "seq")
        if step == 1:
            act_b, gate_b, up_b, back_b = middle_grads(gate_up_b, tie(grads_b, back_a))
            arrived = tie(arrived, back_b)
        if step == 2:
            tokens = tie(jnp.concatenate([tokens_a, tokens_b]), total, normed_full)
            gate_part = across_tokens(tokens, jnp.concatenate([gate_a, gate_b])).astype(low)
            up_part = across_tokens(
                tie(tokens, gate_part), jnp.concatenate([up_a, up_b])
            ).astype(low)
            arrived = tie(arrived, up_part)
        if step == 3:
            inner_act = jnp.concatenate([act_a, act_b])
            down_part = across_tokens(
                tie(inner_act, total), jnp.concatenate([grads_a, grads_b])
            ).astype(low)
            mixed_part = dense_low(tie(inner_act, down_part), down_full).astype(low)
            arrived = tie(arrived, mixed_part)
        total = arrived.astype(jnp.float32) + block_of((back_a, back_b), step + 1).astype(
            jnp.float32
        )
        if step < seq_count - 1:
            total = total.astype(low)
    mixed_halves = (mixed_part[: middle * local_len], mixed_part[middle * local_len :])
    grad_normed_two = total
    mixed = hop(tie(block_of(mixed_halves, 1), arrived), "seq")
    gate_sum = lax.psum_scatter(gate_part, "rows", scatter_dimension=0, tiled=True)
    up_sum = lax.psum_scatter(tie(up_part, gate_part), "rows", scatter_dimension=0, tiled=True)
    grad_out = cotangent[0].astype(jnp.float32)
    gain_two_part = jnp.sum(grad_normed_two * unit_two, axis=0)
    grad_hidden = grad_out + norm_back(grad_normed_two, unit_two, scale_two, gain_two)
    grad_branch = grad_hidden.astype(low)
    grad_attended = against_rows(grad_branch, out_full).astype(low)
    grad_attended = tie(grad_attended, gate_sum)
    gate_blocks = exchange(gate_sum.reshape(seq_count, slab_rows, ff_local), "seq")

    back_q, back_heads, pair_part = attend_back(
        lin, pairs, limits, cosine_t, sine_t, grad_attended, log_totals
    )
    back_q, back_heads, pair_part = tie(
        (back_q, back_heads, pair_part), mixed, *gate_blocks[1:]
    )
    pair_blocks = exchange(pair_part, "seq")
    out_part = across_tokens(tie(attended, pair_blocks[1]), grad_branch).astype(low)
    down_part = tie(down_part, out_part)
    if down_part.shape[0] == out_part.shape[0]:
        out_down = jnp.concatenate([out_part, down_part], axis=1)
        out_down = lax.psum_scatter(out_down, "rows", scatter_dimension=0, tiled=True)
        out_sum, down_grad = out_down[:, :width], out_down[:, width:]
    else:
        out_sum = lax.psum_scatter(out_part, "rows", scatter_dimension=0, tiled=True)
        down_grad = lax.psum_scatter(down_part, "rows", scatter_dimension=0, tiled=True)
    pair_grad = sum_wide(pair_blocks).astype(low)
    back_kv = turn_keys(pair_grad.astype(jnp.float32), -1.0).astype(low)
    kv_heads_first = jnp.transpose(back_kv, (1, 0, 2))
    if row_count == kv_heads:
        lin_back = jnp.concatenate([back_heads, kv_heads_first], axis=2)
    else:
        lin_back = jnp.concatenate(
            [from_heads(back_heads, row_count),
             from_heads(kv_heads_first[:, :, :HEAD_DIM], row_count),
             from_heads(kv_heads_first[:, :, HEAD_DIM:], row_count)], axis=2
        )
    mine = lax.all_to_all(lin_back, "rows", split_axis=0, concat_axis=0, tiled=True)
    mixed = mixed.astype(jnp.float32) + block_of(mixed_halves, 2).astype(jnp.float32)
    mixed = hop(tie(mixed.astype(low), lin_back), "seq")
    up_blocks = exchange(tie(up_sum, lin_back).reshape(seq_count, slab_rows, ff_local), "seq")
    part = across_tokens(normed_full, mine.reshape(-1, mine.shape[-1])).astype(low)
    part = part.reshape(row_count * seq_count, slab_rows, -1)
    part = lax.all_to_all(part, both, split_axis=0, concat_axis=0, tiled=True)
    part_raw = part
    for step in range(3, seq_count):
        mixed = mixed.astype(jnp.float32) + block_of(mixed_halves, step).astype(jnp.float32)
        mixed = hop(tie(mixed.astype(low), part_raw), "seq")
    mixed = mixed.astype(jnp.float32) + block_of(mixed_halves, seq_count).astype(jnp.float32)
    part = part.reshape(row_count, seq_count, slab_rows, -1).astype(jnp.float32)
    proj_grad = jnp.transpose(jnp.sum(part, axis=1), (1, 0, 2))
    query_grad = proj_grad[:, :, :q_split].reshape(-1, q_cols)
    key_grad = proj_grad[:, :, q_split : q_split + kv_split].reshape(-1, kv_cols)
    value_grad = proj_grad[:, :, q_split + kv_split :].reshape(-1, kv_cols)
    layer_out = (hidden_one + mixed).astype(low)
    out_grad = sum_wide(exchange(out_sum.reshape(seq_count, -1, width), "seq"))
    grad_normed = against_rows(
        jnp.concatenate([back_q, back_kv.reshape(local_len, -1)], axis=1), proj_full
    )
    gain_one_part = jnp.sum(grad_normed * unit_one, axis=0)
    input_grad = (
        grad_hidden + norm_back(grad_normed, unit_one, scale_one, gain_one)
    ).astype(low)
    gain_parts = jnp.stack([gain_one_part, gain_two_part], axis=0)
    gain_parts = tie(gain_parts, part_raw)
    gain_parts = jnp.transpose(
        gain_parts.reshape(2, row_count * seq_count, -1), (1, 0, 2)
    )
    gain_sums = jnp.sum(
        lax.all_to_all(gain_parts, both, split_axis=0, concat_axis=0, tiled=True), axis=0
    )
    def owners_rows(blocks):
        whole = in_order(blocks, "seq").astype(jnp.float32)
        whole = whole.reshape(seq_count, slab_rows, row_count, ff_block)
        return jnp.transpose(whole, (1, 2, 0, 3)).reshape(slab_rows, -1)

    gate_grad = owners_rows(tie(tuple(gate_blocks), mine))
    up_grad = owners_rows(up_blocks)
    down_grad = down_grad.astype(jnp.float32)
    return (
        layer_out[None],
        input_grad[None],
        gain_sums[0],
        query_grad,
        key_grad,
        value_grad,
        out_grad,
        gain_sums[1],
        gate_grad,
        up_grad,
        down_grad,
    )


def solution(mesh):
    placed = (
        P("rows", "seq", None),
        P("rows", "seq", None),
        P("rows", None),
        P(("rows", "seq")),
        P(("rows", "seq"), None),
        P(("rows", "seq"), None),
        P(("rows", "seq"), None),
        P(("rows", "seq"), None),
        P(("rows", "seq")),
        P(("rows", "seq"), None),
        P(("rows", "seq"), None),
        P(("rows", "seq"), None),
    )
    return jax.shard_map(
        local,
        mesh=mesh,
        in_specs=placed,
        out_specs=(
            P("rows", "seq", None),
            P("rows", "seq", None),
            P(("rows", "seq")),
            P(("rows", "seq"), None),
            P(("rows", "seq"), None),
            P(("rows", "seq"), None),
            P(("rows", "seq"), None),
            P(("rows", "seq")),
            P(("rows", "seq"), None),
            P(("rows", "seq"), None),
            P(("rows", "seq"), None),
        ),
        check_vma=False,
    )
```

```python
import functools
import math

import jax
import jax.numpy as jnp
from jax import lax
from jax.experimental import pallas as pl
from jax.experimental.pallas import tpu as pltpu
from jax.sharding import PartitionSpec as P

HEAD_DIM = 64
HALF = HEAD_DIM // 2
PAIR = 2 * HEAD_DIM
MEMBERS = 2


epsilon = 1e-05
rope_theta = 500000.0


def rope_table(head_width):
    listed = []
    for column in range(head_width // 2):
        natural = rope_theta ** (-2.0 * column / head_width)
        wavelength = 2.0 * math.pi / natural
        if wavelength > 8192.0:
            scaled = natural / 32.0
        elif wavelength < 2048.0:
            scaled = natural
        else:
            blending = (8192.0 / wavelength - 1.0) / 3.0
            scaled = (1.0 - blending) * natural / 32.0 + blending * natural
        listed.append(scaled)
    return jnp.asarray(listed + listed, dtype=jnp.float32)


def rms_scale(values):
    return lax.rsqrt(jnp.mean(values * values, axis=-1, keepdims=True) + epsilon)


def dense_low(left_side, right_side):
    return jnp.dot(left_side, right_side, preferred_element_type=jnp.float32)


def against_rows(left_side, right_side):
    return lax.dot_general(
        left_side, right_side, (((1,), (1,)), ((), ())), preferred_element_type=jnp.float32
    )


def across_tokens(left_side, right_side):
    return lax.dot_general(
        left_side, right_side, (((0,), (0,)), ((), ())), preferred_element_type=jnp.float32
    )


def norm_back(grad_normed, normed_unit, scale_rows, gain_full):
    scaled_grad = grad_normed * gain_full
    return scale_rows * (
        scaled_grad - normed_unit * jnp.mean(scaled_grad * normed_unit, axis=-1, keepdims=True)
    )


def tie(value, *others):
    return lax.optimization_barrier((value,) + others)[0]


def hop(block, axis, ahead=1):
    count = lax.axis_size(axis)
    return lax.ppermute(block, axis, [(i, (i + ahead) % count) for i in range(count)])


def ring_blocks(own, axis):
    blocks = [own]
    for _ in range(1, lax.axis_size(axis)):
        blocks.append(hop(blocks[-1], axis))
    return blocks


def direct_blocks(own, axis):
    return [own] + [hop(own, axis, ahead) for ahead in range(1, lax.axis_size(axis))]


def exchange(parts, axis):
    count = lax.axis_size(axis)
    here = lax.axis_index(axis)

    def block(ahead):
        return lax.dynamic_index_in_dim(parts, (here + ahead) % count, 0, keepdims=False)

    return [block(0)] + [hop(block(ahead), axis, ahead) for ahead in range(1, count)]


def in_order(blocks, axis):
    count = lax.axis_size(axis)
    here = lax.axis_index(axis)
    out = jnp.zeros((count,) + blocks[0].shape, blocks[0].dtype)
    for back, block in enumerate(blocks):
        out = lax.dynamic_update_index_in_dim(out, block, (here - back + count) % count, 0)
    return out


def sum_wide(blocks):
    return sum((block.astype(jnp.float32) for block in blocks[1:]), blocks[0].astype(jnp.float32))


def dot_of(left, right, left_dim, right_dim):
    return lax.dot_general(
        left, right, (((left_dim,), (right_dim,)), ((), ())), preferred_element_type=jnp.float32
    )


def in_half(block, upper):
    empty = jnp.zeros_like(block)
    return jnp.concatenate([empty, block] if upper else [block, empty], axis=0)


def make_bias(bias_ref, limits_ref):
    keys = lax.broadcasted_iota(jnp.int32, bias_ref.shape, 0)
    allowed = (keys <= limits_ref[0:1, :]) & (keys >= limits_ref[1:2, :])
    bias_ref[...] = jnp.where(allowed, 0.0, -1e30)


def rotated_queries(lin, cosine, sine):
    turned = lin.T
    heads = []
    for top in range(0, turned.shape[0], HEAD_DIM):
        upper, lower = turned[top : top + HALF], turned[top + HALF : top + HEAD_DIM]
        whole = jnp.concatenate(
            [upper * cosine[:HALF] - lower * sine[:HALF], lower * cosine[HALF:] + upper * sine[HALF:]],
            axis=0,
        )
        heads.append(whole.astype(jnp.bfloat16) * jnp.bfloat16(HEAD_DIM**-0.5))
    return heads


def attend_kernel(limits_ref, cos_ref, sin_ref, lin_ref, kv_ref, o_ref, lse_ref, bias_ref, ot_ref):
    @pl.when(pl.program_id(0) == 0)
    def _():
        make_bias(bias_ref, limits_ref)

    q_wide = lin_ref.shape[1] // MEMBERS
    group = q_wide // HEAD_DIM
    for member in range(MEMBERS):
        pair = kv_ref[:, :, member * PAIR : (member + 1) * PAIR].reshape(bias_ref.shape[0], PAIR)
        value = pair.T[HEAD_DIM:]
        lin = lin_ref[:, member * q_wide : (member + 1) * q_wide]
        queries = rotated_queries(lin, cos_ref[...], sin_ref[...])
        for index, query in enumerate(queries):
            head = member * group + index
            scores = dot_of(pair, in_half(query, False), 1, 0) + bias_ref[...]
            highest = jnp.max(scores, axis=0, keepdims=True)
            weights = jnp.exp(scores - highest)
            total = jnp.sum(weights, axis=0, keepdims=True)
            mixed = dot_of(value, weights.astype(jnp.bfloat16), 1, 0) / total
            ot_ref[head * HEAD_DIM : (head + 1) * HEAD_DIM, :] = mixed.astype(jnp.bfloat16)
            lse_ref[head : head + 1, :] = highest + jnp.log(total)
    o_ref[...] = ot_ref[...].T


def attend_back_kernel(
    limits_ref, cos_ref, sin_ref, lin_ref, kv_ref, do_ref, lse_ref,
    dq_ref, dq_heads_ref, dkv_ref, bias_ref, dqt_ref, acc_ref,
):
    @pl.when(pl.program_id(0) == 0)
    def _():
        make_bias(bias_ref, limits_ref)

    q_wide = lin_ref.shape[1] // MEMBERS
    group = q_wide // HEAD_DIM
    cosine, sine = cos_ref[...], sin_ref[...]
    for member in range(MEMBERS):
        lanes = slice(member * PAIR, (member + 1) * PAIR)
        pair = kv_ref[:, :, lanes].reshape(bias_ref.shape[0], PAIR)
        key = pair.T[:HEAD_DIM]
        lin = lin_ref[:, member * q_wide : (member + 1) * q_wide]
        queries = rotated_queries(lin, cosine, sine)
        grads = do_ref[:, member * q_wide : (member + 1) * q_wide].T
        for index, query in enumerate(queries):
            head = member * group + index
            rows = slice(index * HEAD_DIM, (index + 1) * HEAD_DIM)
            query = in_half(query, False)
            grad = in_half(grads[rows], True)
            scores = dot_of(pair, query, 1, 0) + bias_ref[...]
            weights = jnp.exp(scores - lse_ref[head : head + 1, :])
            grad_weights = dot_of(pair, grad, 1, 0)
            centre = jnp.sum(weights * grad_weights, axis=0, keepdims=True)
            grad_scores = (weights * (grad_weights - centre)).astype(jnp.bfloat16)
            back = (dot_of(key, grad_scores, 1, 0) * HEAD_DIM**-0.5).astype(jnp.bfloat16)
            back = back.astype(jnp.float32)
            upper, lower = back[:HALF], back[HALF:]
            dqt_ref[rows, :] = jnp.concatenate(
                [upper * cosine[:HALF] + lower * sine[:HALF],
                 lower * cosine[HALF:] - upper * sine[HALF:]], axis=0,
            ).astype(jnp.bfloat16)
            part = dot_of(grad_scores, query, 1, 1) + dot_of(
                weights.astype(jnp.bfloat16), grad, 1, 1
            )
            if index == 0:
                acc_ref[...] = part
            else:
                acc_ref[...] += part
        turned = dqt_ref[...].T
        dq_ref[:, member * q_wide : (member + 1) * q_wide] = turned
        dq_heads_ref[member] = turned
        dkv_ref[:, :, lanes] = acc_ref[...].astype(jnp.bfloat16).reshape(
            dkv_ref.shape[0], dkv_ref.shape[1], PAIR
        )


def attend_specs(lin, pairs):
    seq_count, tokens, kv_wide = pairs.shape
    kv_heads = kv_wide // PAIR
    q_wide = lin.shape[1] // kv_heads - PAIR
    return kv_heads, q_wide, (
        pl.BlockSpec((2, tokens), lambda i: (0, 0)),
        pl.BlockSpec((HEAD_DIM, tokens), lambda i: (0, 0)),
        pl.BlockSpec((seq_count, tokens, MEMBERS * PAIR), lambda i: (0, 0, i)),
        pl.BlockSpec((tokens, MEMBERS * q_wide), lambda i: (0, i)),
        pl.BlockSpec((MEMBERS * q_wide // HEAD_DIM, tokens), lambda i: (i, 0)),
        pl.BlockSpec((MEMBERS, tokens, q_wide), lambda i: (i, 0, 0)),
    )


def attend(lin, pairs, limits, cosine, sine):
    seq_count, tokens, _ = pairs.shape
    row_len = seq_count * tokens
    kv_heads, q_wide, (limit, table, pair, mixed, stats, _) = attend_specs(lin, pairs)
    q_cols = kv_heads * q_wide
    work = q_cols * tokens * row_len
    return pl.pallas_call(
        attend_kernel,
        grid=(kv_heads // MEMBERS,),
        in_specs=[limit, table, table, mixed, pair],
        out_specs=[mixed, stats],
        out_shape=[
            jax.ShapeDtypeStruct((tokens, q_cols), jnp.bfloat16),
            jax.ShapeDtypeStruct((q_cols // HEAD_DIM, tokens), jnp.float32),
        ],
        scratch_shapes=[
            pltpu.VMEM((row_len, tokens), jnp.float32),
            pltpu.VMEM((MEMBERS * q_wide, tokens), jnp.bfloat16),
        ],
        compiler_params=pltpu.CompilerParams(vmem_limit_bytes=40 * 1024 * 1024),
        cost_estimate=pl.CostEstimate(
            flops=48 * work, bytes_accessed=8 * 1024 * 1024, transcendentals=work // HEAD_DIM
        ),
        name="attend",
    )(limits, cosine, sine, lin, pairs)


def attend_back(lin, pairs, limits, cosine, sine, grads, log_totals):
    seq_count, tokens, _ = pairs.shape
    row_len = seq_count * tokens
    kv_heads, q_wide, (limit, table, pair, mixed, stats, back) = attend_specs(lin, pairs)
    work = kv_heads * q_wide * tokens * row_len
    return pl.pallas_call(
        attend_back_kernel,
        grid=(kv_heads // MEMBERS,),
        in_specs=[limit, table, table, mixed, pair, mixed, stats],
        out_specs=[mixed, back, pair],
        out_shape=[
            jax.ShapeDtypeStruct((tokens, kv_heads * q_wide), jnp.bfloat16),
            jax.ShapeDtypeStruct((kv_heads, tokens, q_wide), jnp.bfloat16),
            jax.ShapeDtypeStruct(pairs.shape, jnp.bfloat16),
        ],
        scratch_shapes=[
            pltpu.VMEM((row_len, tokens), jnp.float32),
            pltpu.VMEM((q_wide, tokens), jnp.bfloat16),
            pltpu.VMEM((row_len, PAIR), jnp.float32),
        ],
        compiler_params=pltpu.CompilerParams(vmem_limit_bytes=40 * 1024 * 1024),
        cost_estimate=pl.CostEstimate(
            flops=72 * work, bytes_accessed=12 * 1024 * 1024, transcendentals=work // HEAD_DIM
        ),
        name="attend_back",
    )(limits, cosine, sine, lin, pairs, grads, log_totals)


def from_heads(lin, count):
    heads, tokens, wide = lin.shape
    if count == heads:
        return lin
    lin = lin.reshape(heads, tokens, count // heads, -1)
    return jnp.transpose(lin, (0, 2, 1, 3)).reshape(count, tokens, -1)


def local(
    inputs,
    cotangent,
    doc_lengths,
    gain_attn,
    w_query,
    w_key,
    w_value,
    w_out,
    gain_mlp,
    w_gate,
    w_up,
    w_down,
):
    seq_count = lax.axis_size("seq")
    row_count = lax.axis_size("rows")
    local_len = inputs.shape[1]
    width = inputs.shape[2]
    row_len = local_len * seq_count
    q_cols, kv_cols = w_query.shape[1], w_key.shape[1]
    q_split, kv_split = q_cols // row_count, kv_cols // row_count
    kv_heads = kv_cols // HEAD_DIM
    slab_rows = w_query.shape[0]
    ff_local = w_gate.shape[1] // seq_count
    ff_block = w_down.shape[0]
    both = ("rows", "seq")
    low = jnp.bfloat16

    q_wide = q_cols // kv_heads
    kv_local = jnp.concatenate(
        [w_key.reshape(-1, kv_heads, HEAD_DIM), w_value.reshape(-1, kv_heads, HEAD_DIM)], axis=2
    ).reshape(slab_rows, -1)
    gains = jnp.pad(jnp.stack([gain_attn, gain_mlp], axis=1), ((0, 0), (0, 126)))
    proj_seq = in_order(
        direct_blocks(jnp.concatenate([w_query, kv_local, gains], axis=1), "seq"), "seq"
    )
    gathered = lax.all_gather(
        proj_seq.reshape(seq_count * slab_rows, -1), "rows", axis=0, tiled=True
    )
    proj_full = gathered[:, : q_cols + 2 * kv_cols]
    gains = gathered[:, q_cols + 2 * kv_cols :].T.astype(jnp.float32)
    gain_one, gain_two = gains[0], gains[1]
    out_seq = in_order(direct_blocks(tie(w_out, proj_seq), "seq"), "seq")
    out_full = lax.all_gather(
        out_seq.reshape(seq_count * slab_rows, -1), "rows", axis=0, tiled=True
    )

    def slab_of(weight):
        cut = weight.reshape(slab_rows, row_count, seq_count, ff_block)
        return jnp.transpose(cut, (2, 0, 1, 3)).reshape(seq_count, slab_rows, ff_local)

    slab = jnp.concatenate([slab_of(w_gate), slab_of(w_up)], axis=2)
    grad_blocks = [cotangent[0], hop(tie(cotangent[0], out_seq), "seq")]
    slab_blocks = exchange(tie(slab, grad_blocks[1]), "seq")

    places = jnp.arange(row_len, dtype=jnp.int32)
    row_lengths = doc_lengths[0]
    doc_ends = jnp.cumsum(row_lengths)
    doc_starts = doc_ends - row_lengths
    inside = (places[:, None] >= doc_starts[None, :]) & (places[:, None] < doc_ends[None, :])
    token_start = jnp.sum(jnp.where(inside, doc_starts[None, :], 0), axis=1)
    offset = lax.axis_index("seq") * local_len
    local_places = lax.dynamic_slice_in_dim(places, offset, local_len)
    local_start = lax.dynamic_slice_in_dim(token_start, offset, local_len)
    limits = jnp.stack([local_places, local_start])
    frequency = rope_table(HEAD_DIM)
    angles = (local_places - local_start).astype(jnp.float32)[:, None] * frequency[None, :]
    cosine, sine = jnp.cos(angles), jnp.sin(angles)
    cosine_t, sine_t = cosine.T, sine.T

    def turn_keys(pair, sign):
        pair = pair.reshape(local_len, kv_heads, PAIR)
        upper, lower, rest = pair[..., :HALF], pair[..., HALF:HEAD_DIM], pair[..., HEAD_DIM:]
        cos_half, sin_half = cosine[:, None, :HALF], sign * sine[:, None, :HALF]
        return jnp.concatenate(
            [upper * cos_half - lower * sin_half, lower * cos_half + upper * sin_half, rest], axis=-1
        )

    inputs_f = inputs[0].astype(jnp.float32)
    scale_one = rms_scale(inputs_f)
    unit_one = inputs_f * scale_one
    normed = (unit_one * gain_one).astype(low)
    lin = dense_low(normed, proj_full)
    pair_local = turn_keys(lin[:, q_cols:], 1.0).astype(low).reshape(local_len, -1)
    slab_blocks = tie(tuple(slab_blocks), pair_local)
    slab = in_order(slab_blocks, "seq").reshape(seq_count * slab_rows, 2 * ff_local)
    gate_up_full = lax.all_gather(slab, "rows", axis=0, tiled=True)
    pairs = in_order(direct_blocks(pair_local, "seq"), "seq")
    down_full = lax.all_gather(tie(w_down, pairs), "rows", axis=0, tiled=True)
    grad_blocks.append(hop(tie(grad_blocks[1], pairs), "seq"))
    attended, log_totals = attend(lin, pairs, limits, cosine_t, sine_t)
    attended = tie(attended, grad_blocks[2])

    hidden_one = inputs_f + dense_low(attended, out_full)
    scale_two = rms_scale(hidden_one)
    unit_two = hidden_one * scale_two
    normed_two = (unit_two * gain_two).astype(low)
    normed_full = lax.all_gather(tie(normed, normed_two), "rows", axis=0, tiled=True)

    middle = seq_count // 2
    blocks = [normed_two]
    for _ in range(1, middle):
        blocks.append(hop(blocks[-1], "seq"))
    tokens_a = jnp.concatenate(blocks)
    gate_up_a = dense_low(tokens_a, gate_up_full)
    blocks.append(hop(blocks[-1], "seq"))
    for step in range(middle + 1, seq_count):
        blocks.append(hop(tie(blocks[-1], gate_up_a) if step == middle + 1 else blocks[-1], "seq"))
    for _ in range(3, seq_count):
        grad_blocks.append(hop(tie(grad_blocks[-1], blocks[-1]), "seq"))
    tokens_b = jnp.concatenate(blocks[middle:])
    gate_up_b = dense_low(tokens_b, gate_up_full)

    def middle_grads(gate_up, grad_block):
        gate_value, up_value = gate_up[:, :ff_local], gate_up[:, ff_local:]
        sigmoid_gate = jax.nn.sigmoid(gate_value)
        act = (gate_value * sigmoid_gate * up_value).astype(low)
        grad_inner = against_rows(grad_block, down_full)
        grad_up = (grad_inner * gate_value * sigmoid_gate).astype(low)
        grad_gate = (
            grad_inner * up_value * sigmoid_gate * (1.0 + gate_value * (1.0 - sigmoid_gate))
        ).astype(low)
        grad_pair = jnp.concatenate([grad_gate, grad_up], axis=1)
        return act, grad_gate, grad_up, against_rows(grad_pair, gate_up_full).astype(low)

    def block_of(halves, step):
        half, place = divmod(step % seq_count, middle)
        return halves[half][place * local_len : (place + 1) * local_len]

    grads_a = jnp.concatenate(grad_blocks[:middle])
    grads_b = jnp.concatenate(grad_blocks[middle:])
    act_a, gate_a, up_a, back_a = middle_grads(gate_up_a, tie(grads_a, gate_up_b))
    total = block_of((back_a,), 1)
    for step in range(1, seq_count):
        arrived = hop(total, "seq")
        if step == 1:
            act_b, gate_b, up_b, back_b = middle_grads(gate_up_b, tie(grads_b, back_a))
            arrived = tie(arrived, back_b)
        if step == 2:
            tokens = tie(jnp.concatenate([tokens_a, tokens_b]), total, normed_full)
            gate_part = across_tokens(tokens, jnp.concatenate([gate_a, gate_b])).astype(low)
            up_part = across_tokens(
                tie(tokens, gate_part), jnp.concatenate([up_a, up_b])
            ).astype(low)
            arrived = tie(arrived, up_part)
        if step == 3:
            inner_act = jnp.concatenate([act_a, act_b])
            down_part = across_tokens(
                tie(inner_act, total), jnp.concatenate([grads_a, grads_b])
            ).astype(low)
            mixed_part = dense_low(tie(inner_act, down_part), down_full).astype(low)
            arrived = tie(arrived, mixed_part)
        total = arrived.astype(jnp.float32) + block_of((back_a, back_b), step + 1).astype(
            jnp.float32
        )
        if step < seq_count - 1:
            total = total.astype(low)
    mixed_halves = (mixed_part[: middle * local_len], mixed_part[middle * local_len :])
    grad_normed_two = total
    mixed = hop(tie(block_of(mixed_halves, 1), arrived), "seq")
    gate_sum = lax.psum_scatter(gate_part, "rows", scatter_dimension=0, tiled=True)
    up_sum = lax.psum_scatter(tie(up_part, gate_part), "rows", scatter_dimension=0, tiled=True)
    grad_out = cotangent[0].astype(jnp.float32)
    gain_two_part = jnp.sum(grad_normed_two * unit_two, axis=0)
    grad_hidden = grad_out + norm_back(grad_normed_two, unit_two, scale_two, gain_two)
    grad_branch = grad_hidden.astype(low)
    grad_attended = against_rows(grad_branch, out_full).astype(low)

    back_q, back_heads, pair_part = attend_back(
        lin, pairs, limits, cosine_t, sine_t, grad_attended, log_totals
    )
    back_q, back_heads, pair_part = tie(
        (back_q, back_heads, pair_part), mixed
    )
    pair_blocks = exchange(pair_part, "seq")
    out_part = across_tokens(tie(attended, pair_blocks[1]), grad_branch).astype(low)
    down_part = tie(down_part, out_part)
    if down_part.shape[0] == out_part.shape[0]:
        out_down = jnp.concatenate([out_part, down_part], axis=1)
        out_down = lax.psum_scatter(out_down, "rows", scatter_dimension=0, tiled=True)
        out_sum, down_grad = out_down[:, :width], out_down[:, width:]
    else:
        out_sum = lax.psum_scatter(out_part, "rows", scatter_dimension=0, tiled=True)
        down_grad = lax.psum_scatter(down_part, "rows", scatter_dimension=0, tiled=True)
    pair_grad = sum_wide(pair_blocks).astype(low)
    back_kv = turn_keys(pair_grad.astype(jnp.float32), -1.0).astype(low)
    kv_heads_first = jnp.transpose(back_kv, (1, 0, 2))
    if row_count == kv_heads:
        lin_back = jnp.concatenate([back_heads, kv_heads_first], axis=2)
    else:
        lin_back = jnp.concatenate(
            [from_heads(back_heads, row_count),
             from_heads(kv_heads_first[:, :, :HEAD_DIM], row_count),
             from_heads(kv_heads_first[:, :, HEAD_DIM:], row_count)], axis=2
        )
    mine = lax.all_to_all(lin_back, "rows", split_axis=0, concat_axis=0, tiled=True)
    mixed = mixed.astype(jnp.float32) + block_of(mixed_halves, 2).astype(jnp.float32)
    mixed = hop(tie(mixed.astype(low), lin_back), "seq")
    gate_blocks = exchange(
        tie(gate_sum, pair_blocks[1]).reshape(seq_count, slab_rows, ff_local), "seq"
    )
    up_blocks = exchange(tie(up_sum, lin_back).reshape(seq_count, slab_rows, ff_local), "seq")
    part = across_tokens(normed_full, mine.reshape(-1, mine.shape[-1])).astype(low)
    part = part.reshape(row_count * seq_count, slab_rows, -1)
    part = lax.all_to_all(part, both, split_axis=0, concat_axis=0, tiled=True)
    part_raw = part
    for step in range(3, seq_count):
        mixed = mixed.astype(jnp.float32) + block_of(mixed_halves, step).astype(jnp.float32)
        mixed = hop(tie(mixed.astype(low), part_raw), "seq")
    mixed = mixed.astype(jnp.float32) + block_of(mixed_halves, seq_count).astype(jnp.float32)
    part = part.reshape(row_count, seq_count, slab_rows, -1).astype(jnp.float32)
    proj_grad = jnp.transpose(jnp.sum(part, axis=1), (1, 0, 2))
    query_grad = proj_grad[:, :, :q_split].reshape(-1, q_cols)
    key_grad = proj_grad[:, :, q_split : q_split + kv_split].reshape(-1, kv_cols)
    value_grad = proj_grad[:, :, q_split + kv_split :].reshape(-1, kv_cols)
    layer_out = (hidden_one + mixed).astype(low)
    out_grad = sum_wide(exchange(out_sum.reshape(seq_count, -1, width), "seq"))
    grad_normed = against_rows(
        jnp.concatenate([back_q, back_kv.reshape(local_len, -1)], axis=1), proj_full
    )
    gain_one_part = jnp.sum(grad_normed * unit_one, axis=0)
    input_grad = (
        grad_hidden + norm_back(grad_normed, unit_one, scale_one, gain_one)
    ).astype(low)
    gain_parts = jnp.stack([gain_one_part, gain_two_part], axis=0)
    gain_parts = tie(gain_parts, part_raw)
    gain_parts = jnp.transpose(
        gain_parts.reshape(2, row_count * seq_count, -1), (1, 0, 2)
    )
    gain_sums = jnp.sum(
        lax.all_to_all(gain_parts, both, split_axis=0, concat_axis=0, tiled=True), axis=0
    )
    def owners_rows(blocks):
        whole = in_order(blocks, "seq").astype(jnp.float32)
        whole = whole.reshape(seq_count, slab_rows, row_count, ff_block)
        return jnp.transpose(whole, (1, 2, 0, 3)).reshape(slab_rows, -1)

    gate_grad = owners_rows(tie(tuple(gate_blocks), mine))
    up_grad = owners_rows(up_blocks)
    down_grad = down_grad.astype(jnp.float32)
    return (
        layer_out[None],
        input_grad[None],
        gain_sums[0],
        query_grad,
        key_grad,
        value_grad,
        out_grad,
        gain_sums[1],
        gate_grad,
        up_grad,
        down_grad,
    )


def solution(mesh):
    placed = (
        P("rows", "seq", None),
        P("rows", "seq", None),
        P("rows", None),
        P(("rows", "seq")),
        P(("rows", "seq"), None),
        P(("rows", "seq"), None),
        P(("rows", "seq"), None),
        P(("rows", "seq"), None),
        P(("rows", "seq")),
        P(("rows", "seq"), None),
        P(("rows", "seq"), None),
        P(("rows", "seq"), None),
    )
    return jax.shard_map(
        local,
        mesh=mesh,
        in_specs=placed,
        out_specs=(
            P("rows", "seq", None),
            P("rows", "seq", None),
            P(("rows", "seq")),
            P(("rows", "seq"), None),
            P(("rows", "seq"), None),
            P(("rows", "seq"), None),
            P(("rows", "seq"), None),
            P(("rows", "seq")),
            P(("rows", "seq"), None),
            P(("rows", "seq"), None),
            P(("rows", "seq"), None),
        ),
        check_vma=False,
    )
```
